256 devices in a mesh: tm: 32 (over z_hi, x, core), tensor: 8 (over z_lo, y).
Axes of the slice: x: 4, y: 4, z: 8 (z_hi: 4, z_lo: 2; z = z_hi * 2 + z_lo), core: 2. Of those that a mesh axis runs over, the one named last changes fastest.
Arguments:
- tokens: bfloat16 [8192, 4096], P('tm', 'tensor'), may hold values from -6 to 6
- w_value: bfloat16 [4096, 4096], P('tm', 'tensor'), may hold values from -0.09375 to 0.09375
- w_gate: bfloat16 [4096, 4096], P('tm', 'tensor'), may hold values from -0.09375 to 0.09375
- filter_taps: bfloat16 [2048, 4096], P(None, 'tensor'), may hold values from -1.1 to 1.1
- w_out: bfloat16 [4096, 4096], P('tensor', 'tm'), may hold values from -0.09375 to 0.09375
Outputs:
- layer_out: bfloat16 [8192, 4096], P('tm', 'tensor')
The draws below stay inside these ranges and needn't reach their ends.
All inputs are finite; a program needn't handle non-finite values.
Results may differ from the reference program's by a relative error of at most 0.023.
Values may be sent and summed in bfloat16 or wider, within the bound.
No kernel may reach another device: no remote copies, remote signals or barrier semaphores. Data moves between devices by JAX's collectives and lax.ppermute only.
A program may use at most 64 MiB of HBM per device.

```python
import math
import jax
import jax.numpy as jnp
from jax import lax

D = 4096
FILT = 2048
TOKENS = 8192
N_TENSOR = 8


def draw_filter_taps(key, part):
    key = jax.random.fold_in(key, 11)
    scale_key, noise_key = jax.random.split(key)
    reach_len = jnp.exp(jax.random.uniform(scale_key, (1, D), jnp.float32, math.log(30.0), math.log(8.0 * FILT)))
    noise_part = jnp.clip(jax.random.normal(noise_key, (FILT, D), jnp.float32), -4.0, 4.0)
    lag_index = jnp.arange(FILT, dtype=jnp.float32)[:, None]
    unit_gain = jnp.sqrt(jnp.expm1(-2.0 / reach_len) / jnp.expm1(-2.0 * FILT / reach_len))
    return (noise_part * jnp.exp(-lag_index / reach_len) * unit_gain).astype(jnp.bfloat16)


def steps_of(key, dims, shards, least, top_value):
    loudness, own = 1.0, jax.random.fold_in(key, 6)
    for axis_at, shards_of in shards:
        steps = jnp.exp(jax.random.uniform(jax.random.fold_in(own, axis_at), (shards_of,), jnp.float32, least / len(shards), top_value / len(shards)))
        loudness = loudness * jnp.repeat(steps, dims[axis_at] // shards_of).reshape([-1 if axis == axis_at else 1 for axis in range(len(dims))])
    return loudness


def gaussian(stream_key, shape, deviation, most, shards=(), held_as=jnp.bfloat16):
    result = deviation * jax.random.normal(stream_key, shape, jnp.float32)
    if shards:
        result = result * steps_of(stream_key, shape, shards, -0.22, 0.18)
    return jnp.clip(result, -most, most).astype(held_as)


def setup_inputs(seed: int = 0) -> dict:
    splits = jax.random.split(jax.random.key(seed), 6)
    return {
        "tokens": gaussian(splits[0], (TOKENS, D), 1.0, 6.0, ((0, 32), (1, 8))),
        "w_value": gaussian(splits[1], (D, D), D ** -0.5, 0.09375, ((0, 32), (1, 8))),
        "w_gate": gaussian(splits[2], (D, D), D ** -0.5, 0.09375, ((0, 32), (1, 8))),
        "filter_taps": draw_filter_taps(jax.random.fold_in(splits[5], 71), 0),
        "w_out": gaussian(splits[4], (D, D), D ** -0.5, 0.09375, ((0, 8), (1, 32))),
    }


def reference(tokens, w_value, w_gate, filter_taps, w_out):
    signal = jnp.dot(tokens, w_value, preferred_element_type=jnp.float32).astype(jnp.bfloat16)
    gate_stream = jnp.dot(tokens, w_gate, preferred_element_type=jnp.float32)
    group_width = math.gcd(D, 256)
    fft_len = TOKENS + FILT

    def convolve_group(group_index):
        offset = group_index * group_width
        part_signal = lax.dynamic_slice_in_dim(signal, offset, group_width, 1).astype(jnp.float32)
        part_taps = lax.dynamic_slice_in_dim(filter_taps, offset, group_width, 1).astype(jnp.float32)
        product = jnp.fft.rfft(part_signal, n=fft_len, axis=0) * jnp.fft.rfft(part_taps, n=fft_len, axis=0)
        return jnp.fft.irfft(product, n=fft_len, axis=0)[:TOKENS]

    pieces = lax.map(convolve_group, jnp.arange(D // group_width, dtype=jnp.int32))
    convolved = jnp.transpose(pieces, (1, 0, 2)).reshape(TOKENS, D)
    gated_mix = (gate_stream * convolved).astype(jnp.bfloat16)
    group_channels = D // N_TENSOR

    def add_group(accumulated, group_index):
        mix_rows = lax.dynamic_slice_in_dim(gated_mix, group_index * group_channels, group_channels, 1)
        weights = lax.dynamic_slice_in_dim(w_out, group_index * group_channels, group_channels, 0)
        partial_value = jnp.dot(mix_rows, weights, preferred_element_type=jnp.float32).astype(jnp.bfloat16)
        partial_value = lax.optimization_barrier(partial_value)
        return accumulated + partial_value.astype(jnp.float32), None

    accumulated, unused = lax.scan(add_group, jnp.zeros((TOKENS, D), jnp.float32), jnp.arange(N_TENSOR, dtype=jnp.int32))
    return accumulated.astype(jnp.bfloat16)
```

```python
import numpy as np
import ml_dtypes
import jax
import jax.numpy as jnp
from jax import lax
from jax.experimental import pallas as pl
from jax.experimental.pallas import tpu as pltpu
from jax.sharding import Mesh, PartitionSpec as P

AXES = ("zh", "x", "c", "zl", "y")
SIZES = {"zh": 4, "x": 4, "c": 2, "zl": 2, "y": 4}
BLOCK = 512
MB = 1 << 20


def split_table(table):
    high = table.astype(ml_dtypes.bfloat16)
    low = (table - high.astype(np.float64)).astype(ml_dtypes.bfloat16)
    return high, low


def dft_tables():
    span = 2 * BLOCK
    k = np.arange(BLOCK)[:, None]
    n = np.arange(BLOCK)[None, :]
    angle = 2.0 * np.pi * ((k * n) % span) / span
    real = np.cos(angle)
    imag = -np.sin(angle)
    imag[0] = np.where(np.arange(BLOCK) % 2 == 0, 1.0, -1.0)
    forward = np.concatenate([real, imag], axis=0)
    scale = np.where(k == 0, 1.0, 2.0) / span
    back_real = np.cos(angle) * scale
    back_imag = -np.sin(angle) * scale
    back_imag[0] = imag[0] / span
    inverse = np.concatenate([back_real, back_imag], axis=0).T
    return split_table(forward), split_table(np.ascontiguousarray(inverse))


def dot(a, b):
    return jnp.dot(a, b, preferred_element_type=jnp.float32)


def shift(block, axis, distance):
    size = SIZES[axis]
    return lax.ppermute(block, axis, [(i, (i + distance) % size) for i in range(size)])


def call(kernel, outs, flops, *args):
    specs = [pl.BlockSpec(memory_space=pltpu.VMEM) for _ in args]
    return pl.pallas_call(
        kernel,
        out_shape=outs,
        in_specs=specs,
        out_specs=jax.tree.map(lambda _: pl.BlockSpec(memory_space=pltpu.VMEM), outs),
        compiler_params=pltpu.CompilerParams(vmem_limit_bytes=40 * MB),
        cost_estimate=pl.CostEstimate(flops=flops, bytes_accessed=4 * MB, transcendentals=0),
    )(*args)


def project_kernel(x_ref, w_ref, o_ref):
    for half in range(2):
        cols = pl.ds(half * 256, 256)
        acc = dot(x_ref[0], w_ref[pl.ds(0, 256), cols])
        for j in range(1, 8):
            acc = acc + dot(x_ref[j], w_ref[pl.ds(j * 256, 256), cols])
        o_ref[:, cols] = acc


def project(x, w):
    return call(project_kernel, jax.ShapeDtypeStruct((512, 512), jnp.float32), 2 * 512 * 2048 * 512, x, w)


def spectra_kernel(taps_ref, high_ref, low_ref, o_ref):
    for s in range(4):
        rows = taps_ref[pl.ds(s * BLOCK, BLOCK), :]
        o_ref[s] = dot(high_ref[...], rows) + dot(low_ref[...], rows)


def conv_kernel(own_ref, d1_ref, d2_ref, d3_ref, d4_ref, taps_ref, high_ref, low_ref, ihigh_ref, ilow_ref, o_ref):
    refs = (own_ref, d1_ref, d2_ref, d3_ref, d4_ref)
    row = lax.broadcasted_iota(jnp.int32, (BLOCK, 256), 0)
    sign = jnp.where(row % 2 == 0, 1.0, -1.0).astype(jnp.float32)
    first = row == 0

    def spectrum(ref):
        rows = ref[...]
        full = dot(high_ref[...], rows) + dot(low_ref[...], rows)
        return full[:BLOCK], full[BLOCK:]

    real = jnp.zeros((BLOCK, 256), jnp.float32)
    imag = jnp.zeros((BLOCK, 256), jnp.float32)
    now = spectrum(refs[0])
    for s in range(4):
        before = spectrum(refs[s + 1])
        vr = now[0] + sign * before[0]
        vi = now[1] + sign * before[1]
        fr = taps_ref[s, pl.ds(0, BLOCK), :]
        fi = taps_ref[s, pl.ds(BLOCK, BLOCK), :]
        cross = fi * vi
        real = real + (fr * vr - jnp.where(first, 0.0, cross))
        imag = imag + jnp.where(first, cross, fr * vi + fi * vr)
        now = before
    out = jnp.zeros((BLOCK, 256), jnp.float32)
    for part, at in ((real, 0), (imag, BLOCK)):
        high = part.astype(jnp.bfloat16)
        low = (part - high.astype(jnp.float32)).astype(jnp.bfloat16)
        cols = pl.ds(at, BLOCK)
        out = out + dot(ihigh_ref[:, cols], high) + dot(ihigh_ref[:, cols], low) + dot(ilow_ref[:, cols], high)
    o_ref[...] = out


def output_kernel(x_ref, w_ref, o_ref):
    x = x_ref[...]
    for j in range(8):
        w = w_ref[pl.ds(2 * j, 2)].reshape(256, 512)
        y = lax.dot_general(x, w, (((1,), (1,)), ((), ())), preferred_element_type=jnp.float32).astype(jnp.bfloat16)
        for core in range(2):
            for block in range(2):
                o_ref[core, j, block] = y[core * 256 : core * 256 + 256, block * 128 : block * 128 + 128]


def local(tokens, w_value, w_gate, filter_taps, w_out):
    (high, low), (ihigh, ilow) = dft_tables()
    zh, x, c, zl, y = (lax.axis_index(a) for a in AXES)
    is0 = c == 0

    def pick(a, b):
        return jnp.where(is0, a, b)

    with jax.named_scope("late_weights"):
        late = jnp.concatenate([w_gate, w_out.T], axis=0)
        late = lax.all_gather(late, ("zh", "x"), axis=0, tiled=False)
        gate_w = late[:, :128].reshape(2048, 512)
        out_w = late[:, 128:]

    with jax.named_scope("value_weights"):
        def gather4(block, axis, at, dim):
            shape = list(block.shape)
            shape.insert(dim, 4)
            buf = jnp.zeros(shape, block.dtype)
            for d in (0, 1, 3, 2):
                got = block if d == 0 else shift(block, axis, d)
                buf = lax.dynamic_update_index_in_dim(buf, got, (at - d) % 4, dim)
            return buf

        value_w = gather4(w_value, "zh", zh, 0)
        value_w = gather4(value_w, "x", x, 1).reshape(2048, 512)

    with jax.named_scope("tokens"):
        t = tokens.reshape(256, 2, 2, 128)
        t0 = t[:, :, 0].reshape(256, 256)
        t1 = t[:, :, 1].reshape(256, 256)
        mine = pick(t0, t1)
        other = shift(pick(t1, t0), "c", 1)
        both = jnp.concatenate([pick(mine, other), pick(other, mine)], axis=0)
        pair = shift(both, "zl", 1)
        low_first = zl == 0
        pair = jnp.stack([jnp.where(low_first, both, pair), jnp.where(low_first, pair, both)])
        features = gather4(pair, "y", y, 1).reshape(8, 512, 256)

    with jax.named_scope("taps"):
        taps = pick(filter_taps[:, :256], filter_taps[:, 256:])
        tap_spectra = call(
            spectra_kernel, jax.ShapeDtypeStruct((4, 1024, 256), jnp.float32), 4 * 4 * 1024 * 512 * 256, taps, high, low
        )

    def across(partial):
        a, b = partial[:, :256], partial[:, 256:]
        return pick(a, b) + shift(pick(b, a), "c", 1)

    with jax.named_scope("signal"):
        signal = across(project(features, value_w)).astype(jnp.bfloat16)

    with jax.named_scope("halo"):
        d4 = lax.ppermute(signal, "zh", [(i, i + 1) for i in range(3)])
        past = [shift(jnp.where(x + d >= 4, d4, signal), "x", d) for d in (1, 2, 3)]

    with jax.named_scope("gate"):
        gate_stream = across(project(features, gate_w))

    with jax.named_scope("conv"):
        convolved = call(
            conv_kernel,
            jax.ShapeDtypeStruct((512, 256), jnp.float32),
            4 * 1024 * 512 * 256 * 6,
            signal, *past, d4, tap_spectra, high, low, ihigh, ilow,
        )

    with jax.named_scope("out"):
        mix = (gate_stream * convolved).astype(jnp.bfloat16)
        theirs = shift(mix, "c", 1)
        mix = jnp.concatenate([pick(mix, theirs), pick(theirs, mix)], axis=1)
        terms = call(
            output_kernel, jax.ShapeDtypeStruct((2, 8, 2, 256, 128), jnp.bfloat16), 2 * 512 * 512 * 2048, mix, out_w
        )
        terms = lax.all_to_all(terms.reshape(16, 2, 256, 128), ("c", "zl", "y"), 0, 0, tiled=True)
        total = terms.reshape(2, 8, 2, 256, 128).astype(jnp.float32).sum(axis=1)
        return total.transpose(2, 1, 0, 3).reshape(256, 512).astype(jnp.bfloat16)


def solution(mesh):
    fine = Mesh(mesh.devices.reshape([SIZES[a] for a in AXES]), AXES)
    tm, tensor = ("zh", "x", "c"), ("zl", "y")
    return jax.shard_map(
        local,
        mesh=fine,
        in_specs=(P(tm, tensor), P(tm, tensor), P(tm, tensor), P(None, tensor), P(tensor, tm)),
        out_specs=P(tm, tensor),
        check_vma=False,
    )
```

```python
import numpy as np
import ml_dtypes
import jax
import jax.numpy as jnp
from jax import lax
from jax.experimental import pallas as pl
from jax.experimental.pallas import tpu as pltpu
from jax.sharding import Mesh, PartitionSpec as P

AXES = ("zh", "x", "c", "zl", "y")
SIZES = {"zh": 4, "x": 4, "c": 2, "zl": 2, "y": 4}
BLOCK = 512
MB = 1 << 20


def split_table(table):
    high = table.astype(ml_dtypes.bfloat16)
    low = (table - high.astype(np.float64)).astype(ml_dtypes.bfloat16)
    return high, low


def dft_tables():
    span = 2 * BLOCK
    k = np.arange(BLOCK)[:, None]
    n = np.arange(BLOCK)[None, :]
    angle = 2.0 * np.pi * ((k * n) % span) / span
    real = np.cos(angle)
    imag = -np.sin(angle)
    imag[0] = np.where(np.arange(BLOCK) % 2 == 0, 1.0, -1.0)
    forward = np.concatenate([real, imag], axis=0)
    scale = np.where(k == 0, 1.0, 2.0) / span
    back_real = np.cos(angle) * scale
    back_imag = -np.sin(angle) * scale
    back_imag[0] = imag[0] / span
    inverse = np.concatenate([back_real, back_imag], axis=0).T
    return split_table(forward), split_table(np.ascontiguousarray(inverse))


def dot(a, b):
    return jnp.dot(a, b, preferred_element_type=jnp.float32)


JOINT = {"zh": ("zh", "c"), "x": ("x", "c"), "y": ("c", "y")}


def shift(block, axis, distance):
    size = SIZES[axis]
    return lax.ppermute(block, axis, [(i, (i + distance) % size) for i in range(size)])


def onward(block, axis):
    def index(i, core):
        return core * 4 + i if JOINT[axis][0] == "c" else i * 2 + core

    pairs = [(index(i, core), index((i + 1 - 2 * core) % 4, core)) for i in range(4) for core in range(2)]
    return lax.ppermute(block, JOINT[axis], pairs)


def ring(block, axis):
    blocks = [block]
    for _ in range(3):
        blocks.append(onward(blocks[-1], axis))
    return blocks


def call(kernel, outs, flops, *args, scratch=(), special=()):
    specs = [pl.BlockSpec(memory_space=pltpu.VMEM) for _ in args]
    for index, spec in special:
        specs[index] = spec
    return pl.pallas_call(
        kernel,
        out_shape=outs,
        grid=(1,),
        in_specs=specs,
        out_specs=jax.tree.map(lambda _: pl.BlockSpec(memory_space=pltpu.VMEM), outs),
        scratch_shapes=list(scratch),
        compiler_params=pltpu.CompilerParams(vmem_limit_bytes=10 * MB),
        cost_estimate=pl.CostEstimate(flops=flops, bytes_accessed=4 * MB, transcendentals=0),
    )(*args)


SCALARS = (0, pl.BlockSpec(memory_space=pltpu.SMEM))


def multiply(x_ref, w_ref, o_ref):
    for half in range(2):
        cols = pl.ds(half * 256, 256)
        acc = jnp.zeros((512, 256), jnp.float32)
        for j in range(8):
            acc = acc + dot(x_ref[j], w_ref[pl.ds(2 * j, 2), :, cols].reshape(256, 256))
        o_ref[:, cols] = acc


def place(at_ref, dz, dx):
    return lax.rem(at_ref[0] + dz + 4, 4) * 4 + lax.rem(at_ref[1] + dx + 4, 4)


def value_kernel(at_ref, w0, w1, w2, w3, t0, t1, t2, t3, o_ref, x_ref, w_ref):
    way = at_ref[4]
    for dx, piece in enumerate((w0, w1, w2, w3)):
        for dz in range(4):
            w_ref[place(at_ref, -dz, dx * way)] = piece[dz]
    for dy, piece in enumerate((t0, t1, t2, t3)):
        y = lax.rem(at_ref[3] + dy * way + 4, 4)
        x_ref[at_ref[2] * 4 + y] = piece[0]
        x_ref[(1 - at_ref[2]) * 4 + y] = piece[1]
    multiply(x_ref, w_ref, o_ref)


def order_late(at_ref, refs, part, w_ref):
    way = at_ref[4]
    for dx in range(4):
        w_ref[place(at_ref, 0, dx * way)] = refs[dx][4 + part]
        for dz in (1, 2, 3):
            w_ref[place(at_ref, dz * way, dx * way)] = refs[4 + dx][dz - 1, part]


def gate_kernel(at_ref, x_ref, *refs):
    o_ref, w_ref = refs[8:]
    order_late(at_ref, refs[:8], 0, w_ref)
    multiply(x_ref, w_ref, o_ref)


def spectra_kernel(taps_ref, high_ref, low_ref, o_ref):
    for s in range(4):
        rows = taps_ref[pl.ds(s * BLOCK, BLOCK), :]
        o_ref[s] = dot(high_ref[...], rows) + dot(low_ref[...], rows)


def conv_kernel(own_ref, d1_ref, d2_ref, d3_ref, d4_ref, taps_ref, high_ref, low_ref, ihigh_ref, ilow_ref, o_ref):
    refs = (own_ref, d1_ref, d2_ref, d3_ref, d4_ref)
    row = lax.broadcasted_iota(jnp.int32, (BLOCK, 256), 0)
    sign = jnp.where(row % 2 == 0, 1.0, -1.0).astype(jnp.float32)
    first = row == 0

    def spectrum(ref):
        rows = ref[...]
        full = dot(high_ref[...], rows) + dot(low_ref[...], rows)
        return full[:BLOCK], full[BLOCK:]

    real = jnp.zeros((BLOCK, 256), jnp.float32)
    imag = jnp.zeros((BLOCK, 256), jnp.float32)
    now = spectrum(refs[0])
    for s in range(4):
        before = spectrum(refs[s + 1])
        vr = now[0] + sign * before[0]
        vi = now[1] + sign * before[1]
        fr = taps_ref[s, pl.ds(0, BLOCK), :]
        fi = taps_ref[s, pl.ds(BLOCK, BLOCK), :]
        cross = fi * vi
        real = real + (fr * vr - jnp.where(first, 0.0, cross))
        imag = imag + jnp.where(first, cross, fr * vi + fi * vr)
        now = before
    out = jnp.zeros((BLOCK, 256), jnp.float32)
    for part, at in ((real, 0), (imag, BLOCK)):
        high = part.astype(jnp.bfloat16)
        low = (part - high.astype(jnp.float32)).astype(jnp.bfloat16)
        cols = pl.ds(at, BLOCK)
        out = out + dot(ihigh_ref[:, cols], high) + dot(ihigh_ref[:, cols], low) + dot(ilow_ref[:, cols], high)
    o_ref[...] = out


def output_kernel(at_ref, x_ref, *refs):
    o_ref, w_ref = refs[8:]
    order_late(at_ref, refs[:8], 1, w_ref)
    x = x_ref[...]
    for j in range(8):
        left, right = w_ref[2 * j], w_ref[2 * j + 1]
        w = jnp.concatenate(
            [jnp.concatenate([b[:, q * 128 : q * 128 + 128] for b in (left, right)], axis=1) for q in range(4)], axis=0
        )
        y = dot(x, w).astype(jnp.bfloat16)
        for core in range(2):
            for block in range(2):
                o_ref[core, j, block] = y[core * 256 : core * 256 + 256, block * 128 : block * 128 + 128]


def local(tokens, w_value, w_gate, filter_taps, w_out):
    (high, low), (ihigh, ilow) = dft_tables()
    zh, x, c, zl, y = (lax.axis_index(a) for a in AXES)
    at = jnp.stack([zh, x, zl, y, 2 * c - 1]).astype(jnp.int32)
    is0 = c == 0
    order = pltpu.VMEM((16, 128, 512), jnp.bfloat16)

    def pick(a, b):
        return jnp.where(is0, a, b)

    with jax.named_scope("stage0"):
        t0 = jnp.concatenate([tokens[:, :128], tokens[:, 256:384]], axis=1)
        t1 = jnp.concatenate([tokens[:, 128:256], tokens[:, 384:]], axis=1)
        mine = pick(t0, t1)
        other = shift(pick(t1, t0), "c", 1)
        own_t = jnp.concatenate([pick(mine, other), pick(other, mine)], axis=0)
        pair = jnp.stack([own_t, shift(own_t, "zl", 1)])
        quarters = [w_out[q * 128 : q * 128 + 128] for q in range(4)]
        late = jnp.stack([w_gate, jnp.concatenate(quarters, axis=1)])
        zs = jnp.stack([w_value] + [shift(w_value, "zh", d) for d in (1, 2, 3)] + [late[0], late[1]])

    with jax.named_scope("stage1"):
        late, pair, zs = lax.optimization_barrier((late, pair, zs))
        values, pairs, lates = [zs], [pair], [late]
        for _ in range(3):
            step = onward(values[-1], "x"), onward(pairs[-1], "y"), onward(lates[-1], "zh")
            step = lax.optimization_barrier(step)
            for blocks, block in zip((values, pairs, lates), step):
                blocks.append(block)

    with jax.named_scope("stage2"):
        fars = [jnp.stack(lates[1:])]
        fars.append(onward(fars[0], "x"))

    def across(partial):
        a, b = partial[:, :256], partial[:, 256:]
        return pick(a, b) + shift(pick(b, a), "c", 1)

    with jax.named_scope("signal"):
        partial, features = call(
            value_kernel,
            (jax.ShapeDtypeStruct((512, 512), jnp.float32), jax.ShapeDtypeStruct((8, 512, 256), jnp.bfloat16)),
            2 * 512 * 2048 * 512,
            at, *values, *pairs, scratch=[order], special=[SCALARS],
        )
        signal = across(partial).astype(jnp.bfloat16)

    with jax.named_scope("halo"):
        d4 = lax.ppermute(signal, "zh", [(i, i + 1) for i in range(3)])
        onwards, _ = lax.optimization_barrier((fars[1], signal))
        fars.append(onward(onwards, "x"))
        past = [shift(jnp.where(x + d >= 4, d4, signal), "x", d) for d in (1, 2, 3)]

        onwards, _ = lax.optimization_barrier((fars[2], d4))
        fars.append(onward(onwards, "x"))

    with jax.named_scope("taps"):
        taps, _ = lax.optimization_barrier((filter_taps, d4))
        taps = pick(taps[:, :256], taps[:, 256:])
        tap_spectra = call(
            spectra_kernel, jax.ShapeDtypeStruct((4, 1024, 256), jnp.float32), 4 * 4 * 1024 * 512 * 256, taps, high, low
        )

    with jax.named_scope("conv"):
        convolved = call(
            conv_kernel,
            jax.ShapeDtypeStruct((512, 256), jnp.float32),
            4 * 1024 * 512 * 256 * 6,
            signal, *past, d4, tap_spectra, high, low, ihigh, ilow,
        )

    with jax.named_scope("gate"):
        features, convolved = lax.optimization_barrier((features, convolved))
        gate_stream = across(
            call(
                gate_kernel, jax.ShapeDtypeStruct((512, 512), jnp.float32), 2 * 512 * 2048 * 512,
                at, features, *values, *fars, scratch=[order], special=[SCALARS],
            )
        )

    with jax.named_scope("out"):
        mix = (gate_stream * convolved).astype(jnp.bfloat16)
        theirs = shift(mix, "c", 1)
        mix = jnp.concatenate([pick(mix, theirs), pick(theirs, mix)], axis=1)
        terms = call(
            output_kernel, jax.ShapeDtypeStruct((2, 8, 2, 256, 128), jnp.bfloat16), 2 * 512 * 512 * 2048,
            at, mix, *values, *fars, scratch=[order], special=[SCALARS],
        )
        terms = lax.all_to_all(terms.reshape(16, 2, 256, 128), ("c", "zl", "y"), 0, 0, tiled=True)
        total = terms.reshape(2, 8, 2, 256, 128).astype(jnp.float32).sum(axis=1)
        return total.transpose(2, 1, 0, 3).reshape(256, 512).astype(jnp.bfloat16)


def solution(mesh):
    fine = Mesh(mesh.devices.reshape([SIZES[a] for a in AXES]), AXES)
    tm, tensor = ("zh", "x", "c"), ("zl", "y")
    return jax.shard_map(
        local,
        mesh=fine,
        in_specs=(P(tm, tensor), P(tm, tensor), P(tm, tensor), P(None, tensor), P(tensor, tm)),
        out_specs=P(tm, tensor),
        check_vma=False,
    )
```

```python
import numpy as np
import ml_dtypes
import jax
import jax.numpy as jnp
from jax import lax
from jax.experimental import pallas as pl
from jax.experimental.pallas import tpu as pltpu
from jax.sharding import Mesh, PartitionSpec as P

AXES = ("zh", "x", "c", "zl", "y")
SIZES = {"zh": 4, "x": 4, "c": 2, "zl": 2, "y": 4}
BLOCK = 512
MB = 1 << 20


def split_table(table):
    high = table.astype(ml_dtypes.bfloat16)
    low = (table - high.astype(np.float64)).astype(ml_dtypes.bfloat16)
    return high, low


def dft_tables():
    span = 2 * BLOCK
    k = np.arange(BLOCK)[:, None]
    n = np.arange(BLOCK)[None, :]
    angle = 2.0 * np.pi * ((k * n) % span) / span
    real = np.cos(angle)
    imag = -np.sin(angle)
    imag[0] = np.where(np.arange(BLOCK) % 2 == 0, 1.0, -1.0)
    forward = np.concatenate([real, imag], axis=0)
    scale = np.where(k == 0, 1.0, 2.0) / span
    back_real = np.cos(angle) * scale
    back_imag = -np.sin(angle) * scale
    back_imag[0] = imag[0] / span
    inverse = np.concatenate([back_real, back_imag], axis=0).T
    return split_table(forward), split_table(np.ascontiguousarray(inverse))


def dot(a, b):
    return jnp.dot(a, b, preferred_element_type=jnp.float32)


JOINT = {"zh": ("zh", "c"), "x": ("x", "c"), "y": ("c", "y")}


def shift(block, axis, distance):
    size = SIZES[axis]
    return lax.ppermute(block, axis, [(i, (i + distance) % size) for i in range(size)])


def onward(block, axis, hops=1):
    def index(i, core):
        return core * 4 + i if JOINT[axis][0] == "c" else i * 2 + core

    pairs = [(index(i, core), index((i + hops * (1 - 2 * core)) % 4, core)) for i in range(4) for core in range(2)]
    return lax.ppermute(block, JOINT[axis], pairs)


def call(kernel, outs, flops, *args, scratch=(), scalars=False):
    specs = [pl.BlockSpec(memory_space=pltpu.VMEM) for _ in args]
    if scalars:
        specs[0] = pl.BlockSpec(memory_space=pltpu.SMEM)
    return pl.pallas_call(
        kernel,
        out_shape=outs,
        in_specs=specs,
        out_specs=jax.tree.map(lambda _: pl.BlockSpec(memory_space=pltpu.VMEM), outs),
        scratch_shapes=list(scratch),
        compiler_params=pltpu.CompilerParams(vmem_limit_bytes=12 * MB),
        cost_estimate=pl.CostEstimate(flops=flops, bytes_accessed=4 * MB, transcendentals=0),
    )(*args)


def multiply(x_ref, w_ref, o_ref):
    for half in range(2):
        cols = pl.ds(half * 256, 256)
        acc = jnp.zeros((512, 256), jnp.float32)
        for j in range(8):
            acc = acc + dot(x_ref[j], w_ref[pl.ds(2 * j, 2), :, cols].reshape(256, 256))
        o_ref[:, cols] = acc


def place(at_ref, dz, dx):
    return lax.rem(at_ref[0] + dz + 4, 4) * 4 + lax.rem(at_ref[1] + dx + 4, 4)


ARRIVALS = {(0, 0): (0, 0, 1), (1, 0): (1, 0, 1), (2, 0): (2, 0, 1), (3, 0): (3, 0, 1), (0, 1): (4, 0, 1)}
ARRIVALS |= {(0, 2): (5, 0, 1), (1, 1): (5, 2, 3), (1, 2): (6, 0, 1), (2, 1): (6, 2, 3)}
ARRIVALS |= {(0, 3): (7, 0, 1), (1, 3): (8, 0, 1), (2, 2): (9, 0, 0), (3, 1): (9, 1, 1)}
ARRIVALS |= {(2, 3): (10, 0, 0), (3, 3): (10, 1, 1), (3, 2): (11, 0, 0)}


def order_arrivals(at_ref, refs, part, w_ref):
    way = at_ref[4]
    for (dz, dx), (arrival, *rows) in ARRIVALS.items():
        w_ref[place(at_ref, dz * way, dx * way)] = refs[arrival][rows[part]]


def value_kernel(at_ref, *refs):
    o_ref, x_ref, w_ref = refs[16:]
    order_arrivals(at_ref, refs[:12], 0, w_ref)
    for dy in range(4):
        y = lax.rem(at_ref[3] + dy * at_ref[4] + 4, 4)
        x_ref[at_ref[2] * 4 + y] = refs[12 + dy][0]
        x_ref[(1 - at_ref[2]) * 4 + y] = refs[12 + dy][1]
    multiply(x_ref, w_ref, o_ref)


def gate_kernel(at_ref, x_ref, *refs):
    o_ref, w_ref = refs[12:]
    order_arrivals(at_ref, refs[:12], 1, w_ref)
    multiply(x_ref, w_ref, o_ref)


def spectra_kernel(taps_ref, high_ref, low_ref, o_ref):
    for s in range(4):
        rows = taps_ref[pl.ds(s * BLOCK, BLOCK), :]
        o_ref[s] = dot(high_ref[...], rows) + dot(low_ref[...], rows)


def conv_kernel(own_ref, d1_ref, d2_ref, d3_ref, d4_ref, taps_ref, high_ref, low_ref, ihigh_ref, ilow_ref, o_ref):
    refs = (own_ref, d1_ref, d2_ref, d3_ref, d4_ref)
    row = lax.broadcasted_iota(jnp.int32, (BLOCK, 256), 0)
    sign = jnp.where(row % 2 == 0, 1.0, -1.0).astype(jnp.float32)
    first = row == 0

    def spectrum(ref):
        rows = ref[...]
        full = dot(high_ref[...], rows) + dot(low_ref[...], rows)
        return full[:BLOCK], full[BLOCK:]

    real = jnp.zeros((BLOCK, 256), jnp.float32)
    imag = jnp.zeros((BLOCK, 256), jnp.float32)
    now = spectrum(refs[0])
    for s in range(4):
        before = spectrum(refs[s + 1])
        vr = now[0] + sign * before[0]
        vi = now[1] + sign * before[1]
        fr = taps_ref[s, pl.ds(0, BLOCK), :]
        fi = taps_ref[s, pl.ds(BLOCK, BLOCK), :]
        cross = fi * vi
        real = real + (fr * vr - jnp.where(first, 0.0, cross))
        imag = imag + jnp.where(first, cross, fr * vi + fi * vr)
        now = before
    out = jnp.zeros((BLOCK, 256), jnp.float32)
    for part, at in ((real, 0), (imag, BLOCK)):
        high = part.astype(jnp.bfloat16)
        low = (part - high.astype(jnp.float32)).astype(jnp.bfloat16)
        cols = pl.ds(at, BLOCK)
        out = out + dot(ihigh_ref[:, cols], high) + dot(ihigh_ref[:, cols], low) + dot(ilow_ref[:, cols], high)
    o_ref[...] = out


def output_kernel(at_ref, x_ref, *refs):
    o_ref, w_ref = refs[10:]
    l0, z2, z3, l3, f1, f2, b0, g, b2, h = refs[:10]
    ways = (
        (l0, f1.at[2], f2.at[4], b0.at[2]),
        (z2.at[2], g.at[2], h.at[1], b2.at[2]),
        (z3.at[2], g.at[3], h.at[2], b2.at[3]),
        (l3, g.at[4], h.at[3], b2.at[4]),
    )
    for dz in range(4):
        for dx in range(4):
            w_ref[place(at_ref, dz * at_ref[4], dx * at_ref[4])] = ways[dz][dx][...]
    x = x_ref[...]
    for j in range(8):
        left, right = w_ref[2 * j], w_ref[2 * j + 1]
        w = jnp.concatenate(
            [jnp.concatenate([b[:, q * 128 : q * 128 + 128] for b in (left, right)], axis=1) for q in range(4)], axis=0
        )
        y = dot(x, w).astype(jnp.bfloat16)
        for core in range(2):
            for block in range(2):
                o_ref[core, j, block] = y[core * 256 : core * 256 + 256, block * 128 : block * 128 + 128]


def local(tokens, w_value, w_gate, filter_taps, w_out):
    (high, low), (ihigh, ilow) = dft_tables()
    zh, x, c, zl, y = (lax.axis_index(a) for a in AXES)
    at = jnp.stack([zh, x, zl, y, 2 * c - 1]).astype(jnp.int32)
    at, is0, wraps, tokens, w_value, w_gate = lax.optimization_barrier(
        (at, c == 0, [x + d >= 4 for d in (1, 2, 3)], tokens, w_value, w_gate)
    )
    order = pltpu.VMEM((16, 128, 512), jnp.bfloat16)

    def pick(a, b):
        return jnp.where(is0, a, b)

    with jax.named_scope("stage0"):
        t0 = jnp.concatenate([tokens[:, :128], tokens[:, 256:384]], axis=1)
        t1 = jnp.concatenate([tokens[:, 128:256], tokens[:, 384:]], axis=1)
        mine = pick(t0, t1)
        other = shift(pick(t1, t0), "c", 1)
        own_t = jnp.concatenate([pick(mine, other), pick(other, mine)], axis=0)
        mixed = jnp.stack([w_value, w_gate])
        quarters = [w_out[q * 128 : q * 128 + 128] for q in range(4)]
        late = jnp.concatenate(quarters, axis=1)
        owns = jnp.stack([w_value, w_gate, late])
        z1, f1, b0, other_t = lax.optimization_barrier(
            (onward(mixed, "zh"), onward(owns, "x"), onward(owns, "x", -1), shift(own_t, "zl", 1))
        )
        pairs = [jnp.stack([own_t, other_t])]

    with jax.named_scope("taps"):
        taps = pick(filter_taps[:, :256], filter_taps[:, 256:])
        tap_spectra = call(
            spectra_kernel, jax.ShapeDtypeStruct((4, 1024, 256), jnp.float32), 4 * 4 * 1024 * 512 * 256, taps, high, low
        )

    with jax.named_scope("stage1"):
        z2, f2, b1, pair = lax.optimization_barrier(
            (
                onward(jnp.concatenate([z1, late[None]]), "zh"),
                onward(jnp.concatenate([f1[:2], z1, f1[2:]]), "x"),
                onward(z1, "x", -1),
                onward(pairs[0], "y"),
            )
        )
        pairs.append(pair)
        z3, f3, pair, tap_spectra = lax.optimization_barrier(
            (onward(z2, "zh"), onward(jnp.concatenate([f2[2:4], z2[:2]]), "x"), onward(pair, "y"), tap_spectra)
        )
        pairs.append(pair)
        f4, b2, pair, direct, l3 = lax.optimization_barrier(
            (
                onward(jnp.stack([f3[2], z3[0]]), "x"),
                onward(jnp.stack([z2[0], z3[0]]), "x", -1),
                onward(pair, "y"),
                onward(z3[:1], "x", 2),
                onward(z3[2], "zh"),
            )
        )
        pairs.append(pair)
        arrivals = (mixed, z1, z2, z3, f1, f2, f3, b0, b1)
        g = onward(jnp.stack([f3[3], z3[1], z2[2], z3[2], l3]), "x")
        b2_late = onward(jnp.stack([z2[1], z3[1], z2[2], z3[2], l3]), "x", -1)

    def across(partial):
        a, b = partial[:, :256], partial[:, 256:]
        return pick(a, b) + shift(pick(b, a), "c", 1)

    with jax.named_scope("signal"):
        partial, features = call(
            value_kernel,
            (jax.ShapeDtypeStruct((512, 512), jnp.float32), jax.ShapeDtypeStruct((8, 512, 256), jnp.bfloat16)),
            2 * 512 * 2048 * 512,
            at, *arrivals, f4, b2, direct, *pairs, scratch=[order], scalars=True,
        )
        signal = across(partial).astype(jnp.bfloat16)

    with jax.named_scope("halo"):
        d4 = lax.ppermute(signal, "zh", [(i, i + 1) for i in range(3)])
        g, b2_late, d4 = lax.optimization_barrier((g, b2_late, d4))
        h = onward(g[1:], "x")
        past = [shift(jnp.where(wraps[d - 1], d4, signal), "x", d) for d in (1, 2, 3)]

    with jax.named_scope("gate"):
        gate_stream = across(
            call(
                gate_kernel, jax.ShapeDtypeStruct((512, 512), jnp.float32), 2 * 512 * 2048 * 512,
                at, features, *arrivals, g, b2_late, h, scratch=[order], scalars=True,
            )
        )

    with jax.named_scope("conv"):
        convolved = call(
            conv_kernel,
            jax.ShapeDtypeStruct((512, 256), jnp.float32),
            4 * 1024 * 512 * 256 * 6,
            signal, *past, d4, tap_spectra, high, low, ihigh, ilow,
        )

    with jax.named_scope("out"):
        mix = (gate_stream * convolved).astype(jnp.bfloat16)
        theirs = shift(mix, "c", 1)
        mix = jnp.concatenate([pick(mix, theirs), pick(theirs, mix)], axis=1)
        terms = call(
            output_kernel, jax.ShapeDtypeStruct((2, 8, 2, 256, 128), jnp.bfloat16), 2 * 512 * 512 * 2048,
            at, mix, late, z2, z3, l3, f1, f2, b0, g, b2_late, h, scratch=[order], scalars=True,
        )
        terms = lax.all_to_all(terms.reshape(16, 2, 256, 128), ("c", "zl", "y"), 0, 0, tiled=True)
        total = terms.reshape(2, 8, 2, 256, 128).astype(jnp.float32).sum(axis=1)
        return total.transpose(2, 1, 0, 3).reshape(256, 512).astype(jnp.bfloat16)


def solution(mesh):
    fine = Mesh(mesh.devices.reshape([SIZES[a] for a in AXES]), AXES)
    tm, tensor = ("zh", "x", "c"), ("zl", "y")
    return jax.shard_map(
        local,
        mesh=fine,
        in_specs=(P(tm, tensor), P(tm, tensor), P(tm, tensor), P(None, tensor), P(tensor, tm)),
        out_specs=P(tm, tensor),
        check_vma=False,
    )
```

```python
import numpy as np
import ml_dtypes
import jax
import jax.numpy as jnp
from jax import lax
from jax.experimental import pallas as pl
from jax.experimental.pallas import tpu as pltpu
from jax.sharding import Mesh, PartitionSpec as P

AXES = ("zh", "x", "c", "zl", "y")
SIZES = {"zh": 4, "x": 4, "c": 2, "zl": 2, "y": 4}
BLOCK = 512
MB = 1 << 20


def split_table(table):
    high = table.astype(ml_dtypes.bfloat16)
    low = (table - high.astype(np.float64)).astype(ml_dtypes.bfloat16)
    return high, low


def dft_tables():
    span = 2 * BLOCK
    k = np.arange(BLOCK)[:, None]
    n = np.arange(BLOCK)[None, :]
    angle = 2.0 * np.pi * ((k * n) % span) / span
    real = np.cos(angle)
    imag = -np.sin(angle)
    imag[0] = np.where(np.arange(BLOCK) % 2 == 0, 1.0, -1.0)
    forward = np.concatenate([real, imag], axis=0)
    scale = np.where(k == 0, 1.0, 2.0) / span
    back_real = np.cos(angle) * scale
    back_imag = -np.sin(angle) * scale
    back_imag[0] = imag[0] / span
    inverse = np.concatenate([back_real, back_imag], axis=0).T
    return split_table(forward), split_table(np.ascontiguousarray(inverse))


def dot(a, b):
    return jnp.dot(a, b, preferred_element_type=jnp.float32)


JOINT = {"zh": ("zh", "c"), "x": ("x", "c"), "y": ("c", "y")}


def shift(block, axis, distance):
    size = SIZES[axis]
    return lax.ppermute(block, axis, [(i, (i + distance) % size) for i in range(size)])


def onward(block, axis, hops=1):
    def index(i, core):
        return core * 4 + i if JOINT[axis][0] == "c" else i * 2 + core

    pairs = [(index(i, core), index((i + hops * (1 - 2 * core)) % 4, core)) for i in range(4) for core in range(2)]
    return lax.ppermute(block, JOINT[axis], pairs)


def call(kernel, outs, flops, *args, scratch=(), scalars=False):
    specs = [pl.BlockSpec(memory_space=pltpu.VMEM) for _ in args]
    if scalars:
        specs[0] = pl.BlockSpec(memory_space=pltpu.SMEM)
    return pl.pallas_call(
        kernel,
        out_shape=outs,
        in_specs=specs,
        out_specs=jax.tree.map(lambda _: pl.BlockSpec(memory_space=pltpu.VMEM), outs),
        scratch_shapes=list(scratch),
        compiler_params=pltpu.CompilerParams(vmem_limit_bytes=12 * MB),
        cost_estimate=pl.CostEstimate(flops=flops, bytes_accessed=4 * MB, transcendentals=0),
    )(*args)


def multiply(x_ref, w_ref, o_ref):
    for half in range(2):
        cols = pl.ds(half * 256, 256)
        acc = jnp.zeros((512, 256), jnp.float32)
        for j in range(8):
            acc = acc + dot(x_ref[j], w_ref[pl.ds(2 * j, 2), :, cols].reshape(256, 256))
        o_ref[:, cols] = acc


def place(at_ref, dz, dx):
    return lax.rem(at_ref[0] + dz + 4, 4) * 4 + lax.rem(at_ref[1] + dx + 4, 4)


ARRIVALS = {(0, 0): (0, 0, 1), (1, 0): (1, 0, 1), (2, 0): (2, 0, 1), (3, 0): (3, 0, 1)}
ARRIVALS |= {(0, 1): (4, 0, 1), (0, 2): (5, 0, 1), (1, 1): (5, 3, 4), (1, 2): (6, 0, 1), (2, 1): (6, 2, 3)}
ARRIVALS |= {(0, 3): (7, 0, 1), (1, 3): (8, 0, 1), (2, 3): (9, 0, 1)}
ARRIVALS |= {(2, 2): (10, 0, 0), (3, 1): (10, 1, 1), (3, 3): (11, 0, 0), (3, 2): (12, 0, 0)}


def order_arrivals(at_ref, refs, part, w_ref):
    way = at_ref[4]
    for (dz, dx), (arrival, *rows) in ARRIVALS.items():
        w_ref[place(at_ref, dz * way, dx * way)] = refs[arrival][rows[part]]


def value_kernel(at_ref, *refs):
    o_ref, x_ref, w_ref = refs[17:]
    order_arrivals(at_ref, refs[:13], 0, w_ref)
    for dy in range(4):
        y = lax.rem(at_ref[3] + dy * at_ref[4] + 4, 4)
        x_ref[at_ref[2] * 4 + y] = refs[13 + dy][0]
        x_ref[(1 - at_ref[2]) * 4 + y] = refs[13 + dy][1]
    multiply(x_ref, w_ref, o_ref)


def gate_kernel(at_ref, x_ref, *refs):
    o_ref, w_ref = refs[13:]
    order_arrivals(at_ref, refs[:13], 1, w_ref)
    multiply(x_ref, w_ref, o_ref)


def spectra_kernel(taps_ref, high_ref, low_ref, o_ref):
    for s in range(4):
        rows = taps_ref[pl.ds(s * BLOCK, BLOCK), :]
        o_ref[s] = dot(high_ref[...], rows) + dot(low_ref[...], rows)


def early_kernel(own_ref, d4_ref, high_ref, low_ref, o_ref):
    for s, ref in enumerate((own_ref, d4_ref)):
        o_ref[s] = dot(high_ref[...], ref[...]) + dot(low_ref[...], ref[...])


def conv_kernel(early_ref, d1_ref, d2_ref, d3_ref, taps_ref, high_ref, low_ref, ihigh_ref, ilow_ref, o_ref):
    refs = (None, d1_ref, d2_ref, d3_ref, None)
    row = lax.broadcasted_iota(jnp.int32, (BLOCK, 256), 0)
    sign = jnp.where(row % 2 == 0, 1.0, -1.0).astype(jnp.float32)
    first = row == 0

    def spectrum(s):
        if s in (0, 4):
            return early_ref[s // 4, pl.ds(0, BLOCK), :], early_ref[s // 4, pl.ds(BLOCK, BLOCK), :]
        rows = refs[s][...]
        full = dot(high_ref[...], rows) + dot(low_ref[...], rows)
        return full[:BLOCK], full[BLOCK:]

    real = jnp.zeros((BLOCK, 256), jnp.float32)
    imag = jnp.zeros((BLOCK, 256), jnp.float32)
    now = spectrum(0)
    for s in range(4):
        before = spectrum(s + 1)
        vr = now[0] + sign * before[0]
        vi = now[1] + sign * before[1]
        fr = taps_ref[s, pl.ds(0, BLOCK), :]
        fi = taps_ref[s, pl.ds(BLOCK, BLOCK), :]
        cross = fi * vi
        real = real + (fr * vr - jnp.where(first, 0.0, cross))
        imag = imag + jnp.where(first, cross, fr * vi + fi * vr)
        now = before
    out = jnp.zeros((BLOCK, 256), jnp.float32)
    for part, at in ((real, 0), (imag, BLOCK)):
        high = part.astype(jnp.bfloat16)
        low = (part - high.astype(jnp.float32)).astype(jnp.bfloat16)
        cols = pl.ds(at, BLOCK)
        out = out + dot(ihigh_ref[:, cols], high) + dot(ihigh_ref[:, cols], low) + dot(ilow_ref[:, cols], high)
    o_ref[...] = out


def output_kernel(at_ref, x_ref, *refs):
    o_ref, w_ref = refs[14:]
    own, z1, z2, z3, f1, f2, f3, b0, b1, b2, g, b3, h, f4 = refs[:14]
    ways = (
        (own.at[2], f1.at[2], f2.at[2], b0.at[2]),
        (z1.at[2], f4.at[2], g.at[2], b1.at[2]),
        (z2.at[2], f4.at[3], g.at[3], b2.at[2]),
        (z3.at[2], g.at[4], h.at[1], b3.at[1]),
    )
    for dz in range(4):
        for dx in range(4):
            w_ref[place(at_ref, dz * at_ref[4], dx * at_ref[4])] = ways[dz][dx][...]
    x = x_ref[...]
    for j in range(8):
        left, right = w_ref[2 * j], w_ref[2 * j + 1]
        w = jnp.concatenate(
            [jnp.concatenate([b[:, q * 128 : q * 128 + 128] for b in (left, right)], axis=1) for q in range(4)], axis=0
        )
        y = dot(x, w).astype(jnp.bfloat16)
        for core in range(2):
            for block in range(2):
                o_ref[core, j, block] = y[core * 256 : core * 256 + 256, block * 128 : block * 128 + 128]


def local(tokens, w_value, w_gate, filter_taps, w_out):
    (high, low), (ihigh, ilow) = dft_tables()
    zh, x, c, zl, y = (lax.axis_index(a) for a in AXES)
    at = jnp.stack([zh, x, zl, y, 2 * c - 1]).astype(jnp.int32)
    at, is0, wraps, tokens, w_value, w_gate = lax.optimization_barrier(
        (at, c == 0, [x + d >= 4 for d in (1, 2, 3)], tokens, w_value, w_gate)
    )
    order = pltpu.VMEM((16, 128, 512), jnp.bfloat16)

    def pick(a, b):
        return jnp.where(is0, a, b)

    with jax.named_scope("stage0"):
        both = jnp.stack([tokens, shift(tokens, "zl", 1)])
        even = jnp.concatenate([both[:, :, :128], both[:, :, 256:384]], axis=2)
        odd = jnp.concatenate([both[:, :, 128:256], both[:, :, 384:]], axis=2)
        mine = pick(even, odd)
        theirs = shift(pick(odd, even), "c", 1)
        quarters = [w_out[q * 128 : q * 128 + 128] for q in range(4)]
        own = jnp.stack([w_value, w_gate, jnp.concatenate(quarters, axis=1)])
        z1, f1, b0, theirs = lax.optimization_barrier(
            (onward(own, "zh"), onward(own, "x"), onward(own, "x", -1), theirs)
        )
        pairs = [jnp.concatenate([pick(mine, theirs), pick(theirs, mine)], axis=1)]

    with jax.named_scope("taps"):
        taps = pick(filter_taps[:, :256], filter_taps[:, 256:])
        tap_spectra = call(
            spectra_kernel, jax.ShapeDtypeStruct((4, 1024, 256), jnp.float32), 4 * 4 * 1024 * 512 * 256, taps, high, low
        )

    with jax.named_scope("stage1"):
        z2, f2, b1, pair = lax.optimization_barrier(
            (
                onward(z1, "zh"),
                onward(jnp.concatenate([f1, z1[:2]]), "x"),
                onward(z1, "x", -1),
                onward(pairs[0], "y"),
            )
        )
        pairs.append(pair)
        z3, f3, b2, pair, tap_spectra = lax.optimization_barrier(
            (
                onward(z2, "zh"),
                onward(jnp.concatenate([f2[3:], z2[:2]]), "x"),
                onward(z2, "x", -1),
                onward(pair, "y"),
                tap_spectra,
            )
        )
        pairs.append(pair)
        f4, b3, pair, direct = lax.optimization_barrier(
            (
                onward(jnp.stack([f3[2], z3[0], z1[2], z2[2]]), "x"),
                onward(z3[:1], "x", -1),
                onward(pair, "y"),
                onward(z3[:1], "x", 2),
            )
        )
        pairs.append(pair)
        arrivals = (own, z1, z2, z3, f1, f2, f3, b0, b1, b2)
        g = onward(jnp.stack([f3[3], z3[1], f4[2], f4[3], z3[2]]), "x")
        b3_late = onward(z3[1:], "x", -1)

    def across(partial):
        a, b = partial[:, :256], partial[:, 256:]
        return pick(a, b) + shift(pick(b, a), "c", 1)

    with jax.named_scope("signal"):
        partial, features = call(
            value_kernel,
            (jax.ShapeDtypeStruct((512, 512), jnp.float32), jax.ShapeDtypeStruct((8, 512, 256), jnp.bfloat16)),
            2 * 512 * 2048 * 512,
            at, *arrivals, f4, b3, direct, *pairs, scratch=[order], scalars=True,
        )
        signal = across(partial).astype(jnp.bfloat16)

    with jax.named_scope("halo"):
        d4 = lax.ppermute(signal, "zh", [(i, i + 1) for i in range(3)])
        past = [shift(jnp.where(wraps[d - 1], d4, signal), "x", d) for d in (1, 2, 3)]

    with jax.named_scope("stage2"):
        early = call(
            early_kernel, jax.ShapeDtypeStruct((2, 1024, 256), jnp.float32), 8 * 1024 * 512 * 256, signal, d4, high, low
        )
        ready, _ = lax.optimization_barrier((g, early))
        h = onward(jnp.stack([ready[1], ready[4]]), "x")

    with jax.named_scope("gate"):
        gate_stream = across(
            call(
                gate_kernel, jax.ShapeDtypeStruct((512, 512), jnp.float32), 2 * 512 * 2048 * 512,
                at, features, *arrivals, g, b3_late, h, scratch=[order], scalars=True,
            )
        )

    with jax.named_scope("conv"):
        convolved = call(
            conv_kernel,
            jax.ShapeDtypeStruct((512, 256), jnp.float32),
            4 * 1024 * 512 * 256 * 6,
            early, *past, tap_spectra, high, low, ihigh, ilow,
        )

    with jax.named_scope("out"):
        mix = (gate_stream * convolved).astype(jnp.bfloat16)
        theirs = shift(mix, "c", 1)
        mix = jnp.concatenate([pick(mix, theirs), pick(theirs, mix)], axis=1)
        terms = call(
            output_kernel, jax.ShapeDtypeStruct((2, 8, 2, 256, 128), jnp.bfloat16), 2 * 512 * 512 * 2048,
            at, mix, *arrivals, g, b3_late, h, f4, scratch=[order], scalars=True,
        )
        terms = lax.all_to_all(terms.reshape(16, 2, 256, 128), ("c", "zl", "y"), 0, 0, tiled=True)
        total = terms.reshape(2, 8, 2, 256, 128).astype(jnp.float32).sum(axis=1)
        return total.transpose(2, 1, 0, 3).reshape(256, 512).astype(jnp.bfloat16)


def solution(mesh):
    fine = Mesh(mesh.devices.reshape([SIZES[a] for a in AXES]), AXES)
    tm, tensor = ("zh", "x", "c"), ("zl", "y")
    return jax.shard_map(
        local,
        mesh=fine,
        in_specs=(P(tm, tensor), P(tm, tensor), P(tm, tensor), P(None, tensor), P(tensor, tm)),
        out_specs=P(tm, tensor),
        check_vma=False,
    )
```

```python
import numpy as np
import ml_dtypes
import jax
import jax.numpy as jnp
from jax import lax
from jax.experimental import pallas as pl
from jax.experimental.pallas import tpu as pltpu
from jax.sharding import Mesh, PartitionSpec as P

AXES = ("zh", "x", "c", "zl", "y")
SIZES = {"zh": 4, "x": 4, "c": 2, "zl": 2, "y": 4}
BLOCK = 512
MB = 1 << 20


def split_table(table):
    high = table.astype(ml_dtypes.bfloat16)
    low = (table - high.astype(np.float64)).astype(ml_dtypes.bfloat16)
    return high, low


def dft_tables():
    span = 2 * BLOCK
    k = np.arange(BLOCK)[:, None]
    n = np.arange(BLOCK)[None, :]
    angle = 2.0 * np.pi * ((k * n) % span) / span
    real = np.cos(angle)
    imag = -np.sin(angle)
    imag[0] = np.where(np.arange(BLOCK) % 2 == 0, 1.0, -1.0)
    forward = np.concatenate([real, imag], axis=0)
    scale = np.where(k == 0, 1.0, 2.0) / span
    back_real = np.cos(angle) * scale
    back_imag = -np.sin(angle) * scale
    back_imag[0] = imag[0] / span
    inverse = np.concatenate([back_real, back_imag], axis=0).T
    return split_table(forward), split_table(np.ascontiguousarray(inverse))


def dot(a, b):
    return jnp.dot(a, b, preferred_element_type=jnp.float32)


JOINT = {"zh": ("zh", "c"), "x": ("x", "c"), "y": ("c", "y")}


def shift(block, axis, distance):
    size = SIZES[axis]
    return lax.ppermute(block, axis, [(i, (i + distance) % size) for i in range(size)])


def onward(block, axis, hops=1):
    def index(i, core):
        return core * 4 + i if JOINT[axis][0] == "c" else i * 2 + core

    pairs = [(index(i, core), index((i + hops * (1 - 2 * core)) % 4, core)) for i in range(4) for core in range(2)]
    return lax.ppermute(block, JOINT[axis], pairs)


def call(kernel, outs, flops, *args, scratch=(), scalars=False):
    specs = [pl.BlockSpec(memory_space=pltpu.VMEM) for _ in args]
    if scalars:
        specs[0] = pl.BlockSpec(memory_space=pltpu.SMEM)
    return pl.pallas_call(
        kernel,
        out_shape=outs,
        in_specs=specs,
        out_specs=jax.tree.map(lambda _: pl.BlockSpec(memory_space=pltpu.VMEM), outs),
        scratch_shapes=list(scratch),
        compiler_params=pltpu.CompilerParams(vmem_limit_bytes=12 * MB),
        cost_estimate=pl.CostEstimate(flops=flops, bytes_accessed=4 * MB, transcendentals=0),
    )(*args)


def multiply(x_ref, w_ref, o_ref):
    for half in range(2):
        cols = pl.ds(half * 256, 256)
        acc = jnp.zeros((512, 256), jnp.float32)
        for j in range(8):
            acc = acc + dot(x_ref[j], w_ref[pl.ds(2 * j, 2), :, cols].reshape(256, 256))
        o_ref[:, cols] = acc


def place(at_ref, dz, dx):
    return lax.rem(at_ref[0] + dz + 4, 4) * 4 + lax.rem(at_ref[1] + dx + 4, 4)


ARRIVALS = {(0, 0): (0, 0, 1), (1, 0): (1, 0, 1), (2, 0): (2, 0, 1), (3, 0): (3, 0, 1)}
ARRIVALS |= {(0, 1): (4, 0, 1), (0, 2): (5, 0, 1), (1, 1): (5, 3, 4), (1, 2): (6, 0, 1), (2, 1): (6, 2, 3)}
ARRIVALS |= {(0, 3): (7, 0, 1), (1, 3): (8, 0, 1), (2, 3): (9, 0, 1)}
ARRIVALS |= {(2, 2): (10, 0, 0), (3, 1): (10, 1, 1), (3, 3): (11, 0, 0), (3, 2): (12, 0, 0)}


def order_arrivals(at_ref, refs, part, w_ref):
    way = at_ref[4]
    for (dz, dx), (arrival, *rows) in ARRIVALS.items():
        w_ref[place(at_ref, dz * way, dx * way)] = refs[arrival][rows[part]]


def columns(x_ref, w_ref, first):
    cols = pl.ds(pl.multiple_of(first, 256), 256)
    acc = jnp.zeros((512, 256), jnp.float32)
    for j in range(8):
        acc = acc + dot(x_ref[j], w_ref[pl.ds(2 * j, 2), :, cols].reshape(256, 256))
    return acc


def theirs_kernel(at_ref, *refs):
    o_ref, x_ref, w_ref = refs[17:]
    order_arrivals(at_ref, refs[:13], 0, w_ref)
    for dy in range(4):
        y = lax.rem(at_ref[3] + dy * at_ref[4] + 4, 4)
        x_ref[at_ref[2] * 4 + y] = refs[13 + dy][0]
        x_ref[(1 - at_ref[2]) * 4 + y] = refs[13 + dy][1]
    o_ref[...] = columns(x_ref, w_ref, at_ref[6])


def mine_kernel(at_ref, x_ref, w_ref, o_ref):
    o_ref[...] = columns(x_ref, w_ref, at_ref[5])


def gate_kernel(at_ref, x_ref, *refs):
    o_ref, w_ref = refs[13:]
    order_arrivals(at_ref, refs[:13], 1, w_ref)
    multiply(x_ref, w_ref, o_ref)


def spectra_kernel(taps_ref, high_ref, low_ref, o_ref):
    for s in range(4):
        rows = taps_ref[pl.ds(s * BLOCK, BLOCK), :]
        o_ref[s] = dot(high_ref[...], rows) + dot(low_ref[...], rows)


def early_kernel(own_ref, d4_ref, high_ref, low_ref, o_ref):
    for s, ref in enumerate((own_ref, d4_ref)):
        o_ref[s] = dot(high_ref[...], ref[...]) + dot(low_ref[...], ref[...])


def conv_kernel(early_ref, d1_ref, d2_ref, d3_ref, taps_ref, high_ref, low_ref, ihigh_ref, ilow_ref, o_ref):
    refs = (None, d1_ref, d2_ref, d3_ref, None)
    row = lax.broadcasted_iota(jnp.int32, (BLOCK, 256), 0)
    sign = jnp.where(row % 2 == 0, 1.0, -1.0).astype(jnp.float32)
    first = row == 0

    def spectrum(s):
        if s in (0, 4):
            return early_ref[s // 4, pl.ds(0, BLOCK), :], early_ref[s // 4, pl.ds(BLOCK, BLOCK), :]
        rows = refs[s][...]
        full = dot(high_ref[...], rows) + dot(low_ref[...], rows)
        return full[:BLOCK], full[BLOCK:]

    real = jnp.zeros((BLOCK, 256), jnp.float32)
    imag = jnp.zeros((BLOCK, 256), jnp.float32)
    now = spectrum(0)
    for s in range(4):
        before = spectrum(s + 1)
        vr = now[0] + sign * before[0]
        vi = now[1] + sign * before[1]
        fr = taps_ref[s, pl.ds(0, BLOCK), :]
        fi = taps_ref[s, pl.ds(BLOCK, BLOCK), :]
        cross = fi * vi
        real = real + (fr * vr - jnp.where(first, 0.0, cross))
        imag = imag + jnp.where(first, cross, fr * vi + fi * vr)
        now = before
    out = jnp.zeros((BLOCK, 256), jnp.float32)
    for part, at in ((real, 0), (imag, BLOCK)):
        high = part.astype(jnp.bfloat16)
        low = (part - high.astype(jnp.float32)).astype(jnp.bfloat16)
        cols = pl.ds(at, BLOCK)
        out = out + dot(ihigh_ref[:, cols], high) + dot(ihigh_ref[:, cols], low) + dot(ilow_ref[:, cols], high)
    o_ref[...] = out


def output_kernel(at_ref, x_ref, *refs):
    o_ref, w_ref = refs[15:]
    own, z1, z2, z3, f1, f2, f3, b0, b1, b2, g, b3, h, f4, l3 = refs[:15]
    ways = (
        (own.at[2], f1.at[2], f2.at[2], b0.at[2]),
        (z2.at[2], f4.at[2], g.at[2], b2.at[2]),
        (z3.at[2], f4.at[3], g.at[3], b3.at[1]),
        (l3, g.at[4], h.at[1], b3.at[2]),
    )
    for dz in range(4):
        for dx in range(4):
            w_ref[place(at_ref, dz * at_ref[4], dx * at_ref[4])] = ways[dz][dx][...]
    x = x_ref[...]
    for j in range(8):
        left, right = w_ref[2 * j], w_ref[2 * j + 1]
        w = jnp.concatenate(
            [jnp.concatenate([b[:, q * 128 : q * 128 + 128] for b in (left, right)], axis=1) for q in range(4)], axis=0
        )
        y = dot(x, w).astype(jnp.bfloat16)
        for core in range(2):
            for block in range(2):
                o_ref[core, j, block] = y[core * 256 : core * 256 + 256, block * 128 : block * 128 + 128]


def local(tokens, w_value, w_gate, filter_taps, w_out):
    (high, low), (ihigh, ilow) = dft_tables()
    zh, x, c, zl, y = (lax.axis_index(a) for a in AXES)
    at = jnp.stack([zh, x, zl, y, 2 * c - 1, 256 * c, 256 - 256 * c]).astype(jnp.int32)
    at, is0, wraps, tokens, w_value, w_gate = lax.optimization_barrier(
        (at, c == 0, [x + d >= 4 for d in (1, 2, 3)], tokens, w_value, w_gate)
    )
    order = pltpu.VMEM((16, 128, 512), jnp.bfloat16)

    def pick(a, b):
        return jnp.where(is0, a, b)

    with jax.named_scope("stage0"):
        both = jnp.stack([tokens, shift(tokens, "zl", 1)])
        even = jnp.concatenate([both[:, :, :128], both[:, :, 256:384]], axis=2)
        odd = jnp.concatenate([both[:, :, 128:256], both[:, :, 384:]], axis=2)
        mine = pick(even, odd)
        theirs = shift(pick(odd, even), "c", 1)
        quarters = [w_out[q * 128 : q * 128 + 128] for q in range(4)]
        own = jnp.stack([w_value, w_gate, jnp.concatenate(quarters, axis=1)])
        z1, f1, b0, theirs = lax.optimization_barrier(
            (onward(own[:2], "zh"), onward(own, "x"), onward(own, "x", -1), theirs)
        )
        pairs = [jnp.concatenate([pick(mine, theirs), pick(theirs, mine)], axis=1)]

    with jax.named_scope("taps"):
        taps = pick(filter_taps[:, :256], filter_taps[:, 256:])
        tap_spectra = call(
            spectra_kernel, jax.ShapeDtypeStruct((4, 1024, 256), jnp.float32), 4 * 4 * 1024 * 512 * 256, taps, high, low
        )

    with jax.named_scope("stage1"):
        z2, f2, b1, pair = lax.optimization_barrier(
            (
                onward(jnp.concatenate([z1, own[2:]]), "zh"),
                onward(jnp.concatenate([f1, z1]), "x"),
                onward(z1, "x", -1),
                onward(pairs[0], "y"),
            )
        )
        pairs.append(pair)
        z3, f3, b2, pair, tap_spectra = lax.optimization_barrier(
            (
                onward(z2, "zh"),
                onward(jnp.concatenate([f2[3:], z2[:2]]), "x"),
                onward(z2, "x", -1),
                onward(pair, "y"),
                tap_spectra,
            )
        )
        pairs.append(pair)
        f4, b3, pair, direct, l3 = lax.optimization_barrier(
            (
                onward(jnp.stack([f3[2], z3[0], z2[2], z3[2]]), "x"),
                onward(z3[:1], "x", -1),
                onward(pair, "y"),
                onward(z3[:1], "x", 2),
                onward(z3[2], "zh"),
            )
        )
        pairs.append(pair)
        arrivals = (own, z1, z2, z3, f1, f2, f3, b0, b1, b2)
        g = onward(jnp.stack([f3[3], z3[1], f4[2], f4[3], l3]), "x")
        b3_late = onward(jnp.stack([z3[1], z3[2], l3]), "x", -1)

    def across(partial):
        a, b = partial[:, :256], partial[:, 256:]
        return pick(a, b) + shift(pick(b, a), "c", 1)

    with jax.named_scope("signal"):
        half = jax.ShapeDtypeStruct((512, 256), jnp.float32)
        theirs, features, ordered = call(
            theirs_kernel,
            (half, jax.ShapeDtypeStruct((8, 512, 256), jnp.bfloat16), jax.ShapeDtypeStruct((16, 128, 512), jnp.bfloat16)),
            512 * 2048 * 512,
            at, *arrivals, f4, b3, direct, *pairs, scalars=True,
        )
        theirs = shift(theirs, "c", 1)
        mine = call(mine_kernel, half, 512 * 2048 * 512, at, features, ordered, scalars=True)
        signal = (mine + theirs).astype(jnp.bfloat16)

    with jax.named_scope("halo"):
        d4 = lax.ppermute(signal, "zh", [(i, i + 1) for i in range(3)])
        past = [shift(jnp.where(wraps[d - 1], d4, signal), "x", d) for d in (1, 2, 3)]

    with jax.named_scope("stage2"):
        early = call(
            early_kernel, jax.ShapeDtypeStruct((2, 1024, 256), jnp.float32), 8 * 1024 * 512 * 256, signal, d4, high, low
        )
        ready, _ = lax.optimization_barrier((g, d4))
        h = onward(jnp.stack([ready[1], ready[4]]), "x")

    with jax.named_scope("gate"):
        gate_stream = across(
            call(
                gate_kernel, jax.ShapeDtypeStruct((512, 512), jnp.float32), 2 * 512 * 2048 * 512,
                at, features, *arrivals, g, b3_late, h, scratch=[order], scalars=True,
            )
        )

    with jax.named_scope("conv"):
        convolved = call(
            conv_kernel,
            jax.ShapeDtypeStruct((512, 256), jnp.float32),
            4 * 1024 * 512 * 256 * 6,
            early, *past, tap_spectra, high, low, ihigh, ilow,
        )

    with jax.named_scope("out"):
        mix = (gate_stream * convolved).astype(jnp.bfloat16)
        theirs = shift(mix, "c", 1)
        mix = jnp.concatenate([pick(mix, theirs), pick(theirs, mix)], axis=1)
        terms = call(
            output_kernel, jax.ShapeDtypeStruct((2, 8, 2, 256, 128), jnp.bfloat16), 2 * 512 * 512 * 2048,
            at, mix, *arrivals, g, b3_late, h, f4, l3, scratch=[order], scalars=True,
        )
        terms = lax.all_to_all(terms.reshape(16, 2, 256, 128), ("c", "zl", "y"), 0, 0, tiled=True)
        total = terms.reshape(2, 8, 2, 256, 128).astype(jnp.float32).sum(axis=1)
        return total.transpose(2, 1, 0, 3).reshape(256, 512).astype(jnp.bfloat16)


def solution(mesh):
    fine = Mesh(mesh.devices.reshape([SIZES[a] for a in AXES]), AXES)
    tm, tensor = ("zh", "x", "c"), ("zl", "y")
    return jax.shard_map(
        local,
        mesh=fine,
        in_specs=(P(tm, tensor), P(tm, tensor), P(tm, tensor), P(None, tensor), P(tensor, tm)),
        out_specs=P(tm, tensor),
        check_vma=False,
    )
```

```python
import numpy as np
import ml_dtypes
import jax
import jax.numpy as jnp
from jax import lax
from jax.experimental import pallas as pl
from jax.experimental.pallas import tpu as pltpu
from jax.sharding import Mesh, PartitionSpec as P

AXES = ("zh", "x", "c", "zl", "y")
SIZES = {"zh": 4, "x": 4, "c": 2, "zl": 2, "y": 4}
BLOCK = 512
MB = 1 << 20


def split_table(table):
    high = table.astype(ml_dtypes.bfloat16)
    low = (table - high.astype(np.float64)).astype(ml_dtypes.bfloat16)
    return high, low


def dft_tables():
    span = 2 * BLOCK
    k = np.arange(BLOCK)[:, None]
    n = np.arange(BLOCK)[None, :]
    angle = 2.0 * np.pi * ((k * n) % span) / span
    real = np.cos(angle)
    imag = -np.sin(angle)
    imag[0] = np.where(np.arange(BLOCK) % 2 == 0, 1.0, -1.0)
    forward = np.concatenate([real, imag], axis=0)
    scale = np.where(k == 0, 1.0, 2.0) / span
    back_real = np.cos(angle) * scale
    back_imag = -np.sin(angle) * scale
    back_imag[0] = imag[0] / span
    inverse = np.concatenate([back_real, back_imag], axis=0).T
    return split_table(forward), split_table(np.ascontiguousarray(inverse))


def dot(a, b):
    return jnp.dot(a, b, preferred_element_type=jnp.float32)


JOINT = {"zh": ("zh", "c"), "x": ("x", "c"), "y": ("c", "y")}


def shift(block, axis, distance):
    size = SIZES[axis]
    return lax.ppermute(block, axis, [(i, (i + distance) % size) for i in range(size)])


def onward(block, axis, hops=1):
    def index(i, core):
        return core * 4 + i if JOINT[axis][0] == "c" else i * 2 + core

    pairs = [(index(i, core), index((i + hops * (1 - 2 * core)) % 4, core)) for i in range(4) for core in range(2)]
    return lax.ppermute(block, JOINT[axis], pairs)


def call(kernel, outs, flops, *args, scratch=(), scalars=False):
    specs = [pl.BlockSpec(memory_space=pltpu.VMEM) for _ in args]
    if scalars:
        specs[0] = pl.BlockSpec(memory_space=pltpu.SMEM)
    return pl.pallas_call(
        kernel,
        out_shape=outs,
        in_specs=specs,
        out_specs=jax.tree.map(lambda _: pl.BlockSpec(memory_space=pltpu.VMEM), outs),
        scratch_shapes=list(scratch),
        compiler_params=pltpu.CompilerParams(vmem_limit_bytes=12 * MB),
        cost_estimate=pl.CostEstimate(flops=flops, bytes_accessed=4 * MB, transcendentals=0),
    )(*args)


def multiply(x_ref, w_ref, o_ref):
    for half in range(2):
        cols = pl.ds(half * 256, 256)
        acc = jnp.zeros((512, 256), jnp.float32)
        for j in range(8):
            acc = acc + dot(x_ref[j], w_ref[pl.ds(2 * j, 2), :, cols].reshape(256, 256))
        o_ref[:, cols] = acc


def place(at_ref, dz, dx):
    return lax.rem(at_ref[0] + dz + 4, 4) * 4 + lax.rem(at_ref[1] + dx + 4, 4)


ARRIVALS = {(0, 0): (0, 0, 1), (1, 0): (1, 0, 1), (2, 0): (2, 0, 1), (3, 0): (3, 0, 1)}
ARRIVALS |= {(0, 1): (4, 0, 1), (0, 2): (5, 0, 1), (1, 1): (5, 3, 4), (1, 2): (6, 0, 1), (2, 1): (6, 2, 3)}
ARRIVALS |= {(0, 3): (7, 0, 1), (1, 3): (8, 0, 1), (2, 3): (9, 0, 1)}
ARRIVALS |= {(2, 2): (10, 0, 0), (3, 1): (10, 1, 1), (3, 3): (11, 0, 0), (3, 2): (12, 0, 0)}


def order_arrivals(at_ref, refs, part, w_ref):
    way = at_ref[4]
    for (dz, dx), (arrival, *rows) in ARRIVALS.items():
        w_ref[place(at_ref, dz * way, dx * way)] = refs[arrival][rows[part]]


def columns(x_ref, w_ref, first):
    cols = pl.ds(pl.multiple_of(first, 256), 256)
    acc = jnp.zeros((512, 256), jnp.float32)
    for j in range(8):
        acc = acc + dot(x_ref[j], w_ref[pl.ds(2 * j, 2), :, cols].reshape(256, 256))
    return acc


def theirs_kernel(at_ref, *refs):
    o_ref, x_ref, w_ref = refs[17:]
    order_arrivals(at_ref, refs[:13], 0, w_ref)
    for dy in range(4):
        y = lax.rem(at_ref[3] + dy * at_ref[4] + 4, 4)
        x_ref[at_ref[2] * 4 + y] = refs[13 + dy][0]
        x_ref[(1 - at_ref[2]) * 4 + y] = refs[13 + dy][1]
    o_ref[...] = columns(x_ref, w_ref, at_ref[6])


def mine_kernel(at_ref, x_ref, w_ref, o_ref):
    o_ref[...] = columns(x_ref, w_ref, at_ref[5])


def gate_kernel(at_ref, x_ref, *refs):
    o_ref, w_ref = refs[13:]
    order_arrivals(at_ref, refs[:13], 1, w_ref)
    multiply(x_ref, w_ref, o_ref)


def spectra_kernel(taps_ref, high_ref, low_ref, o_ref):
    for s in range(4):
        rows = taps_ref[pl.ds(s * BLOCK, BLOCK), :]
        o_ref[s] = dot(high_ref[...], rows) + dot(low_ref[...], rows)


def early_kernel(own_ref, d4_ref, high_ref, low_ref, o_ref):
    for s, ref in enumerate((own_ref, d4_ref)):
        o_ref[s] = dot(high_ref[...], ref[...]) + dot(low_ref[...], ref[...])


def conv_kernel(early_ref, d1_ref, d2_ref, d3_ref, taps_ref, high_ref, low_ref, ihigh_ref, ilow_ref, o_ref):
    refs = (None, d1_ref, d2_ref, d3_ref, None)
    row = lax.broadcasted_iota(jnp.int32, (BLOCK, 256), 0)
    sign = jnp.where(row % 2 == 0, 1.0, -1.0).astype(jnp.float32)
    first = row == 0

    def spectrum(s):
        if s in (0, 4):
            return early_ref[s // 4, pl.ds(0, BLOCK), :], early_ref[s // 4, pl.ds(BLOCK, BLOCK), :]
        rows = refs[s][...]
        full = dot(high_ref[...], rows) + dot(low_ref[...], rows)
        return full[:BLOCK], full[BLOCK:]

    real = jnp.zeros((BLOCK, 256), jnp.float32)
    imag = jnp.zeros((BLOCK, 256), jnp.float32)
    now = spectrum(0)
    for s in range(4):
        before = spectrum(s + 1)
        vr = now[0] + sign * before[0]
        vi = now[1] + sign * before[1]
        fr = taps_ref[s, pl.ds(0, BLOCK), :]
        fi = taps_ref[s, pl.ds(BLOCK, BLOCK), :]
        cross = fi * vi
        real = real + (fr * vr - jnp.where(first, 0.0, cross))
        imag = imag + jnp.where(first, cross, fr * vi + fi * vr)
        now = before
    out = jnp.zeros((BLOCK, 256), jnp.float32)
    for part, at in ((real, 0), (imag, BLOCK)):
        high = part.astype(jnp.bfloat16)
        low = (part - high.astype(jnp.float32)).astype(jnp.bfloat16)
        cols = pl.ds(at, BLOCK)
        out = out + dot(ihigh_ref[:, cols], high) + dot(ihigh_ref[:, cols], low) + dot(ilow_ref[:, cols], high)
    o_ref[...] = out


def output_weights_kernel(at_ref, *refs):
    own, z1, z2, z3, f1, f2, f3, b0, b1, b2, g, b3, h, f4, l3 = refs[:15]
    o_ref, w_ref = refs[15:]
    ways = (
        (own.at[2], f1.at[2], f2.at[2], b0.at[2]),
        (z2.at[2], f4.at[2], g.at[2], b2.at[2]),
        (z3.at[2], f4.at[3], g.at[3], b3.at[1]),
        (l3, g.at[4], h.at[1], b3.at[2]),
    )
    for dz in range(4):
        for dx in range(4):
            w_ref[place(at_ref, dz * at_ref[4], dx * at_ref[4])] = ways[dz][dx][...]
    for j in range(8):
        for block in range(2):
            for q in range(4):
                rows, cols = pl.ds(q * 128, 128), pl.ds(block * 128, 128)
                o_ref[j, rows, cols] = w_ref[2 * j + block, :, q * 128 : q * 128 + 128]


def output_kernel(x_ref, w_ref, o_ref):
    x = x_ref[...]
    for j in range(8):
        y = dot(x, w_ref[j]).astype(jnp.bfloat16)
        for core in range(2):
            for block in range(2):
                o_ref[core, j, block] = y[core * 256 : core * 256 + 256, block * 128 : block * 128 + 128]


def local(tokens, w_value, w_gate, filter_taps, w_out):
    (high, low), (ihigh, ilow) = dft_tables()
    zh, x, c, zl, y = (lax.axis_index(a) for a in AXES)
    at = jnp.stack([zh, x, zl, y, 2 * c - 1, 256 * c, 256 - 256 * c]).astype(jnp.int32)
    at, is0, wraps, tokens, w_value, w_gate = lax.optimization_barrier(
        (at, c == 0, [x + d >= 4 for d in (1, 2, 3)], tokens, w_value, w_gate)
    )
    order = pltpu.VMEM((16, 128, 512), jnp.bfloat16)

    def pick(a, b):
        return jnp.where(is0, a, b)

    with jax.named_scope("stage0"):
        both = jnp.stack([tokens, shift(tokens, "zl", 1)])
        even = jnp.concatenate([both[:, :, :128], both[:, :, 256:384]], axis=2)
        odd = jnp.concatenate([both[:, :, 128:256], both[:, :, 384:]], axis=2)
        mine = pick(even, odd)
        theirs = shift(pick(odd, even), "c", 1)
        quarters = [w_out[q * 128 : q * 128 + 128] for q in range(4)]
        own = jnp.stack([w_value, w_gate, jnp.concatenate(quarters, axis=1)])
        z1, f1, b0, theirs = lax.optimization_barrier(
            (onward(own[:2], "zh"), onward(own, "x"), onward(own, "x", -1), theirs)
        )
        pairs = [jnp.concatenate([pick(mine, theirs), pick(theirs, mine)], axis=1)]

    with jax.named_scope("taps"):
        taps = pick(filter_taps[:, :256], filter_taps[:, 256:])
        tap_spectra = call(
            spectra_kernel, jax.ShapeDtypeStruct((4, 1024, 256), jnp.float32), 4 * 4 * 1024 * 512 * 256, taps, high, low
        )

    with jax.named_scope("stage1"):
        b1 = onward(z1, "x", -1)
        z2, f2, pair = lax.optimization_barrier(
            (
                onward(jnp.concatenate([z1, own[2:]]), "zh"),
                onward(jnp.concatenate([f1, z1]), "x"),
                onward(pairs[0], "y"),
            )
        )
        pairs.append(pair)
        z3, f3, b1, b2, pair, tap_spectra = lax.optimization_barrier(
            (
                onward(z2, "zh"),
                onward(jnp.concatenate([f2[3:], z2[:2]]), "x"),
                b1,
                onward(z2, "x", -1),
                onward(pair, "y"),
                tap_spectra,
            )
        )
        pairs.append(pair)
        f4, b3, pair, direct, l3 = lax.optimization_barrier(
            (
                onward(jnp.stack([f3[2], z3[0], z2[2], z3[2]]), "x"),
                onward(z3[:1], "x", -1),
                onward(pair, "y"),
                onward(z3[:1], "x", 2),
                onward(z3[2], "zh"),
            )
        )
        pairs.append(pair)
        arrivals = (own, z1, z2, z3, f1, f2, f3, b0, b1, b2)
        g = onward(jnp.stack([f3[3], z3[1], f4[2], f4[3], l3]), "x")
        b3_late = onward(jnp.stack([z3[1], z3[2], l3]), "x", -1)

    def across(partial):
        a, b = partial[:, :256], partial[:, 256:]
        return pick(a, b) + shift(pick(b, a), "c", 1)

    with jax.named_scope("signal"):
        half = jax.ShapeDtypeStruct((512, 256), jnp.float32)
        theirs, features, ordered = call(
            theirs_kernel,
            (half, jax.ShapeDtypeStruct((8, 512, 256), jnp.bfloat16), jax.ShapeDtypeStruct((16, 128, 512), jnp.bfloat16)),
            512 * 2048 * 512,
            at, *arrivals, f4, b3, direct, *pairs, scalars=True,
        )
        theirs = shift(theirs, "c", 1)
        mine = call(mine_kernel, half, 512 * 2048 * 512, at, features, ordered, scalars=True)
        signal = (mine + theirs).astype(jnp.bfloat16)

    with jax.named_scope("halo"):
        d4 = lax.ppermute(signal, "zh", [(i, i + 1) for i in range(3)])
        past = [shift(jnp.where(wraps[d - 1], d4, signal), "x", d) for d in (1, 2, 3)]

    with jax.named_scope("stage2"):
        early = call(
            early_kernel, jax.ShapeDtypeStruct((2, 1024, 256), jnp.float32), 8 * 1024 * 512 * 256, signal, d4, high, low
        )
        ready, _ = lax.optimization_barrier((g, d4))
        h = onward(jnp.stack([ready[1], ready[4]]), "x")

    with jax.named_scope("gate"):
        gate_stream = across(
            call(
                gate_kernel, jax.ShapeDtypeStruct((512, 512), jnp.float32), 2 * 512 * 2048 * 512,
                at, features, *arrivals, g, b3_late, h, scratch=[order], scalars=True,
            )
        )

    with jax.named_scope("out_weights"):
        out_w = call(
            output_weights_kernel, jax.ShapeDtypeStruct((8, 512, 256), jnp.bfloat16), 512 * 512 * 2048,
            at, *arrivals, g, b3_late, h, f4, l3, scratch=[order], scalars=True,
        )
        early, out_w = lax.optimization_barrier((early, out_w))

    with jax.named_scope("conv"):
        convolved = call(
            conv_kernel,
            jax.ShapeDtypeStruct((512, 256), jnp.float32),
            4 * 1024 * 512 * 256 * 24,
            early, *past, tap_spectra, high, low, ihigh, ilow,
        )

    with jax.named_scope("out"):
        mix = (gate_stream * convolved).astype(jnp.bfloat16)
        theirs = shift(mix, "c", 1)
        mix = jnp.concatenate([pick(mix, theirs), pick(theirs, mix)], axis=1)
        terms = call(
            output_kernel, jax.ShapeDtypeStruct((2, 8, 2, 256, 128), jnp.bfloat16), 2 * 512 * 512 * 2048,
            mix, out_w,
        )
        terms = lax.all_to_all(terms.reshape(16, 2, 256, 128), ("c", "zl", "y"), 0, 0, tiled=True)
        total = terms.reshape(2, 8, 2, 256, 128).astype(jnp.float32).sum(axis=1)
        return total.transpose(2, 1, 0, 3).reshape(256, 512).astype(jnp.bfloat16)


def solution(mesh):
    fine = Mesh(mesh.devices.reshape([SIZES[a] for a in AXES]), AXES)
    tm, tensor = ("zh", "x", "c"), ("zl", "y")
    return jax.shard_map(
        local,
        mesh=fine,
        in_specs=(P(tm, tensor), P(tm, tensor), P(tm, tensor), P(None, tensor), P(tensor, tm)),
        out_specs=P(tm, tensor),
        check_vma=False,
    )
```

```python
import numpy as np
import ml_dtypes
import jax
import jax.numpy as jnp
from jax import lax
from jax.experimental import pallas as pl
from jax.experimental.pallas import tpu as pltpu
from jax.sharding import Mesh, PartitionSpec as P

AXES = ("zh", "x", "c", "zl", "y")
SIZES = {"zh": 4, "x": 4, "c": 2, "zl": 2, "y": 4}
BLOCK = 512
MB = 1 << 20


def split_table(table):
    high = table.astype(ml_dtypes.bfloat16)
    low = (table - high.astype(np.float64)).astype(ml_dtypes.bfloat16)
    return high, low


def dft_tables():
    span = 2 * BLOCK
    k = np.arange(BLOCK)[:, None]
    n = np.arange(BLOCK)[None, :]
    angle = 2.0 * np.pi * ((k * n) % span) / span
    real = np.cos(angle)
    imag = -np.sin(angle)
    imag[0] = np.where(np.arange(BLOCK) % 2 == 0, 1.0, -1.0)
    forward = np.concatenate([real, imag], axis=0)
    scale = np.where(k == 0, 1.0, 2.0) / span
    back_real = np.cos(angle) * scale
    back_imag = -np.sin(angle) * scale
    back_imag[0] = imag[0] / span
    inverse = np.concatenate([back_real, back_imag], axis=0).T
    return split_table(forward), split_table(np.ascontiguousarray(inverse))


def dot(a, b):
    return jnp.dot(a, b, preferred_element_type=jnp.float32)


JOINT = {"zh": ("zh", "c"), "x": ("x", "c"), "y": ("c", "y")}


def shift(block, axis, distance):
    size = SIZES[axis]
    return lax.ppermute(block, axis, [(i, (i + distance) % size) for i in range(size)])


def onward(block, axis, hops=1):
    def index(i, core):
        return core * 4 + i if JOINT[axis][0] == "c" else i * 2 + core

    pairs = [(index(i, core), index((i + hops * (1 - 2 * core)) % 4, core)) for i in range(4) for core in range(2)]
    return lax.ppermute(block, JOINT[axis], pairs)


def call(kernel, outs, flops, *args, scratch=(), scalars=False):
    specs = [pl.BlockSpec(memory_space=pltpu.VMEM) for _ in args]
    if scalars:
        specs[0] = pl.BlockSpec(memory_space=pltpu.SMEM)
    return pl.pallas_call(
        kernel,
        out_shape=outs,
        in_specs=specs,
        out_specs=jax.tree.map(lambda _: pl.BlockSpec(memory_space=pltpu.VMEM), outs),
        scratch_shapes=list(scratch),
        compiler_params=pltpu.CompilerParams(vmem_limit_bytes=12 * MB),
        cost_estimate=pl.CostEstimate(flops=flops, bytes_accessed=4 * MB, transcendentals=0),
    )(*args)


def multiply(x_ref, w_ref, o_ref):
    for half in range(2):
        cols = pl.ds(half * 256, 256)
        acc = jnp.zeros((512, 256), jnp.float32)
        for j in range(8):
            acc = acc + dot(x_ref[j], w_ref[pl.ds(2 * j, 2), :, cols].reshape(256, 256))
        o_ref[:, cols] = acc


def place(at_ref, dz, dx):
    return lax.rem(at_ref[0] + dz + 4, 4) * 4 + lax.rem(at_ref[1] + dx + 4, 4)


ARRIVALS = {(0, 0): (0, 0, 1), (1, 0): (1, 0, 1), (2, 0): (2, 0, 1), (3, 0): (3, 0, 1)}
ARRIVALS |= {(0, 1): (4, 0, 1), (0, 2): (5, 0, 1), (1, 1): (5, 3, 4), (1, 2): (6, 0, 1), (2, 1): (6, 2, 3)}
ARRIVALS |= {(0, 3): (7, 0, 1), (1, 3): (8, 0, 1), (2, 3): (9, 0, 1)}
ARRIVALS |= {(2, 2): (10, 0, 0), (3, 1): (10, 1, 1), (3, 3): (11, 0, 0), (3, 2): (12, 0, 0)}


def order_arrivals(at_ref, refs, part, w_ref):
    way = at_ref[4]
    for (dz, dx), (arrival, *rows) in ARRIVALS.items():
        w_ref[place(at_ref, dz * way, dx * way)] = refs[arrival][rows[part]]


def columns(x_ref, w_ref, first):
    cols = pl.ds(pl.multiple_of(first, 256), 256)
    acc = jnp.zeros((512, 256), jnp.float32)
    for j in range(8):
        acc = acc + dot(x_ref[j], w_ref[pl.ds(2 * j, 2), :, cols].reshape(256, 256))
    return acc


def theirs_kernel(at_ref, *refs):
    o_ref, x_ref, w_ref = refs[17:]
    order_arrivals(at_ref, refs[:13], 0, w_ref)
    for dy in range(4):
        y = lax.rem(at_ref[3] + dy * at_ref[4] + 4, 4)
        x_ref[at_ref[2] * 4 + y] = refs[13 + dy][0]
        x_ref[(1 - at_ref[2]) * 4 + y] = refs[13 + dy][1]
    o_ref[...] = columns(x_ref, w_ref, at_ref[6])


def mine_kernel(at_ref, x_ref, w_ref, o_ref):
    o_ref[...] = columns(x_ref, w_ref, at_ref[5])


def gate_kernel(at_ref, x_ref, *refs):
    o_ref, w_ref = refs[13:]
    order_arrivals(at_ref, refs[:13], 1, w_ref)
    multiply(x_ref, w_ref, o_ref)


def spectra_kernel(taps_ref, high_ref, low_ref, o_ref):
    for s in range(4):
        rows = taps_ref[pl.ds(s * BLOCK, BLOCK), :]
        o_ref[s] = dot(high_ref[...], rows) + dot(low_ref[...], rows)


def early_kernel(own_ref, d4_ref, high_ref, low_ref, o_ref):
    for s, ref in enumerate((own_ref, d4_ref)):
        o_ref[s] = dot(high_ref[...], ref[...]) + dot(low_ref[...], ref[...])


def conv_kernel(gate_ref, early_ref, d1_ref, d2_ref, d3_ref, taps_ref, high_ref, low_ref, ihigh_ref, ilow_ref, o_ref):
    refs = (None, d1_ref, d2_ref, d3_ref, None)
    row = lax.broadcasted_iota(jnp.int32, (BLOCK, 256), 0)
    sign = jnp.where(row % 2 == 0, 1.0, -1.0).astype(jnp.float32)
    first = row == 0

    def spectrum(s):
        if s in (0, 4):
            return early_ref[s // 4, pl.ds(0, BLOCK), :], early_ref[s // 4, pl.ds(BLOCK, BLOCK), :]
        rows = refs[s][...]
        full = dot(high_ref[...], rows) + dot(low_ref[...], rows)
        return full[:BLOCK], full[BLOCK:]

    real = jnp.zeros((BLOCK, 256), jnp.float32)
    imag = jnp.zeros((BLOCK, 256), jnp.float32)
    now = spectrum(0)
    for s in range(4):
        before = spectrum(s + 1)
        vr = now[0] + sign * before[0]
        vi = now[1] + sign * before[1]
        fr = taps_ref[s, pl.ds(0, BLOCK), :]
        fi = taps_ref[s, pl.ds(BLOCK, BLOCK), :]
        cross = fi * vi
        real = real + (fr * vr - jnp.where(first, 0.0, cross))
        imag = imag + jnp.where(first, cross, fr * vi + fi * vr)
        now = before
    out = jnp.zeros((BLOCK, 256), jnp.float32)
    for part, at in ((real, 0), (imag, BLOCK)):
        high = part.astype(jnp.bfloat16)
        low = (part - high.astype(jnp.float32)).astype(jnp.bfloat16)
        cols = pl.ds(at, BLOCK)
        out = out + dot(ihigh_ref[:, cols], high) + dot(ihigh_ref[:, cols], low) + dot(ilow_ref[:, cols], high)
    o_ref[...] = (gate_ref[...] * out).astype(jnp.bfloat16)


def output_weights_kernel(at_ref, *refs):
    own, z1, z2, z3, f1, f2, f3, b0, b1, b2, g, b3, h, f4, l3 = refs[:15]
    o_ref, w_ref = refs[15:]
    ways = (
        (own.at[2], f1.at[2], f2.at[2], b0.at[2]),
        (z2.at[2], f4.at[2], g.at[2], b2.at[2]),
        (z3.at[2], f4.at[3], g.at[3], b3.at[1]),
        (l3, g.at[4], h.at[1], b3.at[2]),
    )
    for dz in range(4):
        for dx in range(4):
            w_ref[place(at_ref, dz * at_ref[4], dx * at_ref[4])] = ways[dz][dx][...]
    for j in range(8):
        for block in range(2):
            for q in range(4):
                rows, cols = pl.ds(q * 128, 128), pl.ds(block * 128, 128)
                o_ref[j, rows, cols] = w_ref[2 * j + block, :, q * 128 : q * 128 + 128]


def output_kernel(x_ref, w_ref, o_ref):
    x = x_ref[...]
    for j in range(8):
        y = dot(x, w_ref[j]).astype(jnp.bfloat16)
        for core in range(2):
            for block in range(2):
                o_ref[core, j, block] = y[core * 256 : core * 256 + 256, block * 128 : block * 128 + 128]


def sum_kernel(t_ref, o_ref):
    for core in range(2):
        for block in range(2):
            total = t_ref[core * 8, block].astype(jnp.float32)
            for group in range(1, 8):
                total = total + t_ref[core * 8 + group, block].astype(jnp.float32)
            o_ref[:, pl.ds((2 * block + core) * 128, 128)] = total.astype(jnp.bfloat16)


def local(tokens, w_value, w_gate, filter_taps, w_out):
    (high, low), (ihigh, ilow) = dft_tables()
    zh, x, c, zl, y = (lax.axis_index(a) for a in AXES)
    at = jnp.stack([zh, x, zl, y, 2 * c - 1, 256 * c, 256 - 256 * c]).astype(jnp.int32)
    at, is0, wraps, tokens, w_value, w_gate = lax.optimization_barrier(
        (at, c == 0, [x + d >= 4 for d in (1, 2, 3)], tokens, w_value, w_gate)
    )
    order = pltpu.VMEM((16, 128, 512), jnp.bfloat16)

    def pick(a, b):
        return jnp.where(is0, a, b)

    with jax.named_scope("stage0"):
        both = jnp.stack([tokens, shift(tokens, "zl", 1)])
        even = jnp.concatenate([both[:, :, :128], both[:, :, 256:384]], axis=2)
        odd = jnp.concatenate([both[:, :, 128:256], both[:, :, 384:]], axis=2)
        mine = pick(even, odd)
        theirs = shift(pick(odd, even), "c", 1)
        quarters = [w_out[q * 128 : q * 128 + 128] for q in range(4)]
        own = jnp.stack([w_value, w_gate, jnp.concatenate(quarters, axis=1)])
        z1, f1, b0, theirs = lax.optimization_barrier(
            (onward(own[:2], "zh"), onward(own, "x"), onward(own, "x", -1), theirs)
        )
        pairs = [jnp.concatenate([pick(mine, theirs), pick(theirs, mine)], axis=1)]

    with jax.named_scope("taps"):
        taps = pick(filter_taps[:, :256], filter_taps[:, 256:])
        tap_spectra = call(
            spectra_kernel, jax.ShapeDtypeStruct((4, 1024, 256), jnp.float32), 4 * 4 * 1024 * 512 * 256, taps, high, low
        )

    with jax.named_scope("stage1"):
        b1 = onward(z1, "x", -1)
        z2, f2, pair = lax.optimization_barrier(
            (
                onward(jnp.concatenate([z1, own[2:]]), "zh"),
                onward(jnp.concatenate([f1, z1]), "x"),
                onward(pairs[0], "y"),
            )
        )
        pairs.append(pair)
        z3, f3, b1, b2, pair, tap_spectra = lax.optimization_barrier(
            (
                onward(z2, "zh"),
                onward(jnp.concatenate([f2[3:], z2[:2]]), "x"),
                b1,
                onward(z2, "x", -1),
                onward(pair, "y"),
                tap_spectra,
            )
        )
        pairs.append(pair)
        f4, b3, pair, direct, l3 = lax.optimization_barrier(
            (
                onward(jnp.stack([f3[2], z3[0], z2[2], z3[2]]), "x"),
                onward(z3[:1], "x", -1),
                onward(pair, "y"),
                onward(z3[:1], "x", 2),
                onward(z3[2], "zh"),
            )
        )
        pairs.append(pair)
        arrivals = (own, z1, z2, z3, f1, f2, f3, b0, b1, b2)
        g = onward(jnp.stack([f3[3], z3[1], f4[2], f4[3], l3]), "x")
        b3_late = onward(jnp.stack([z3[1], z3[2], l3]), "x", -1)

    def across(partial):
        a, b = partial[:, :256], partial[:, 256:]
        return pick(a, b) + shift(pick(b, a), "c", 1)

    with jax.named_scope("signal"):
        half = jax.ShapeDtypeStruct((512, 256), jnp.float32)
        theirs, features, ordered = call(
            theirs_kernel,
            (half, jax.ShapeDtypeStruct((8, 512, 256), jnp.bfloat16), jax.ShapeDtypeStruct((16, 128, 512), jnp.bfloat16)),
            512 * 2048 * 512,
            at, *arrivals, f4, b3, direct, *pairs, scalars=True,
        )
        theirs = shift(theirs, "c", 1)
        mine = call(mine_kernel, half, 512 * 2048 * 512, at, features, ordered, scalars=True)
        signal = (mine + theirs).astype(jnp.bfloat16)

    with jax.named_scope("halo"):
        d4 = lax.ppermute(signal, "zh", [(i, i + 1) for i in range(3)])
        past = [shift(jnp.where(wraps[d - 1], d4, signal), "x", d) for d in (1, 2, 3)]

    with jax.named_scope("stage2"):
        early = call(
            early_kernel, jax.ShapeDtypeStruct((2, 1024, 256), jnp.float32), 8 * 1024 * 512 * 256, signal, d4, high, low
        )
        ready, _ = lax.optimization_barrier((g, d4))
        h = onward(jnp.stack([ready[1], ready[4]]), "x")

    with jax.named_scope("gate"):
        gate_stream = across(
            call(
                gate_kernel, jax.ShapeDtypeStruct((512, 512), jnp.float32), 2 * 512 * 2048 * 512,
                at, features, *arrivals, g, b3_late, h, scratch=[order], scalars=True,
            )
        )

    with jax.named_scope("out_weights"):
        out_w = call(
            output_weights_kernel, jax.ShapeDtypeStruct((8, 512, 256), jnp.bfloat16), 512 * 512 * 2048,
            at, *arrivals, g, b3_late, h, f4, l3, scratch=[order], scalars=True,
        )
        early, out_w = lax.optimization_barrier((early, out_w))

    with jax.named_scope("conv"):
        mix = call(
            conv_kernel,
            jax.ShapeDtypeStruct((512, 256), jnp.bfloat16),
            4 * 1024 * 512 * 256 * 24,
            gate_stream, early, *past, tap_spectra, high, low, ihigh, ilow,
        )

    with jax.named_scope("out"):
        theirs = shift(mix, "c", 1)
        mix = jnp.concatenate([pick(mix, theirs), pick(theirs, mix)], axis=1)
        terms = call(
            output_kernel, jax.ShapeDtypeStruct((2, 8, 2, 256, 128), jnp.bfloat16), 2 * 512 * 512 * 2048,
            mix, out_w,
        )
        terms = lax.all_to_all(terms.reshape(16, 2, 256, 128), ("c", "zl", "y"), 0, 0, tiled=True)
        return call(sum_kernel, jax.ShapeDtypeStruct((256, 512), jnp.bfloat16), 16 * 256 * 256, terms)


def solution(mesh):
    fine = Mesh(mesh.devices.reshape([SIZES[a] for a in AXES]), AXES)
    tm, tensor = ("zh", "x", "c"), ("zl", "y")
    return jax.shard_map(
        local,
        mesh=fine,
        in_specs=(P(tm, tensor), P(tm, tensor), P(tm, tensor), P(None, tensor), P(tensor, tm)),
        out_specs=P(tm, tensor),
        check_vma=False,
    )
```
